32 devices in a mesh: rep: 4 (over y, x), blk: 8 (over z, core).
Axes of the slice: x: 2, y: 2, z: 4, core: 2. Of those that a mesh axis runs over, the one named last changes fastest.
Arguments:
- node_features: bfloat16 [8192, 256], P(('rep', 'blk')), may hold values from -6 to 6
- tile_values: bfloat16 [4, 8, 16, 128, 128], P('rep', 'blk'), may hold values from -0.25 to 0.25
- tile_row: int32 [4, 8, 16], P('rep', 'blk'), may hold values from 0 to 7, as said below
- tile_col: int32 [4, 8, 16], P('rep', 'blk'), may hold values from 0 to 15
- tile_count: int32 [4, 8], P('rep', 'blk'), may hold values from 2 to 16, as said below
- weight: bfloat16 [256, 256], replicated, may hold values from -0.375 to 0.375
- cotangent: bfloat16 [8, 4, 256, 256], P('blk', 'rep'), may hold values from -6 to 6
Outputs:
- layer_out: bfloat16 [8, 4, 256, 256], P('blk', 'rep')
- grad_weight: float32 [256, 256], replicated
- grad_features: bfloat16 [8192, 256], P(('rep', 'blk'))
The draws below stay inside these ranges and needn't reach their ends.
Inputs may be any that keep to these rules, and one draw needn't show every extreme that they name: `tile_row`: within one device the live slots name distinct tile pairs. Slots 0 to tile_count - 1 of a device are live, the rest are ignored; some device has all 16 slots live.
All inputs are finite; a program needn't handle non-finite values.
Results may differ from the reference program's by a relative error of at most 0.03.
Values may be sent and summed in bfloat16 or wider, within the bound.
A program may use at most 128 MiB of HBM per device.

```python
import jax
import jax.numpy as jnp
from jax import lax

F = 256
TILE = 128
XR = 256
SLAB = 1024
GROUP = 2048
SLAB_BLOCKS = 8
GROUP_BLOCKS = 16
TILES_DEV = 16
NODES = 8192
N_REP = 4
N_BLK = 8


def tile_pairs(key):
    pair_key = jax.random.fold_in(key, 7)

    def one_device(device_index):
        return jax.random.permutation(jax.random.fold_in(pair_key, device_index), SLAB_BLOCKS * GROUP_BLOCKS)[:TILES_DEV]
    chosen = jax.vmap(one_device)(jnp.arange(N_REP * N_BLK, dtype=jnp.int32))
    return chosen.reshape(N_REP, N_BLK, TILES_DEV).astype(jnp.int32)


def draw_tile_row(key, part):
    return (tile_pairs(key) // GROUP_BLOCKS).astype(jnp.int32)


def draw_tile_col(key, part):
    return (tile_pairs(key) % GROUP_BLOCKS).astype(jnp.int32)


def draw_tile_count(key, part):
    halvings = jax.random.randint(jax.random.fold_in(key, 11), (N_REP * N_BLK,), 0, 4)
    counts = jnp.maximum(TILES_DEV // 2 ** halvings, 1)
    fullest = jax.random.randint(jax.random.fold_in(key, 13), (), 0, N_REP * N_BLK)
    counts = jnp.where(jnp.arange(N_REP * N_BLK, dtype=jnp.int32) == fullest, TILES_DEV, counts)
    return counts.reshape(N_REP, N_BLK).astype(jnp.int32)


def block_scale(key, shape, shards, smallest, largest):
    def one(dim, shards_of):
        heights = jax.random.uniform(jax.random.fold_in(jax.random.fold_in(key, 6), dim), (shards_of,), jnp.float32, smallest / len(shards), largest / len(shards))
        return jnp.repeat(jnp.exp(heights), shape[dim] // shards_of).reshape((-1,) + (1,) * (len(shape) - dim - 1))

    gain = one(*shards[0])
    for cut in shards[1:]:
        gain = gain * one(*cut)
    return gain


def centred(rng, extent, scale, reach, split=(), kind=jnp.bfloat16):
    gain = block_scale(rng, extent, split, -0.22, 0.18) if split else 1.0
    values = jax.random.normal(rng, extent, jnp.float32) * scale * gain
    return jnp.minimum(jnp.maximum(values, -reach), reach).astype(kind)


def setup_inputs(seed: int = 0) -> dict:
    arg_keys = jax.random.split(jax.random.key(seed), 8)
    return {
        "node_features": centred(arg_keys[0], (NODES, F), 1.0, 6.0, ((0, 32),)),
        "tile_values": centred(arg_keys[1], (N_REP, N_BLK, TILES_DEV, TILE, TILE), (TILE * TILES_DEV * N_REP // (2 * SLAB_BLOCKS)) ** -0.5, 0.25, ((0, 4), (1, 8))),
        "tile_row": draw_tile_row(jax.random.fold_in(arg_keys[7], 71), 0),
        "tile_col": draw_tile_col(jax.random.fold_in(arg_keys[7], 71), 0),
        "tile_count": draw_tile_count(jax.random.fold_in(arg_keys[7], 71), 0),
        "weight": centred(arg_keys[5], (F, F), F ** -0.5, 0.375),
        "cotangent": centred(arg_keys[6], (N_BLK, N_REP, XR, F), 1.0, 6.0, ((0, 8), (1, 4))),
    }


def reference(node_features, tile_values, tile_row, tile_col, tile_count, weight, cotangent):
    groups = node_features.reshape(N_REP, GROUP_BLOCKS, TILE, F)
    live_mask = (jnp.arange(TILES_DEV, dtype=jnp.int32)[None, None, :] < tile_count[:, :, None]).astype(jnp.float32)
    row_hot = (tile_row[..., None] == jnp.arange(SLAB_BLOCKS, dtype=jnp.int32)).astype(jnp.float32) * live_mask[..., None]
    col_hot = (tile_col[..., None] == jnp.arange(GROUP_BLOCKS, dtype=jnp.int32)).astype(jnp.float32) * live_mask[..., None]

    def forward_slab(slab_index):
        def one_group(group_index):
            picked = jnp.take(groups[group_index], tile_col[group_index, slab_index], axis=0)
            products = jnp.einsum('tij,tjf->tif', tile_values[group_index, slab_index].astype(jnp.float32), picked.astype(jnp.float32))
            partial_value = jnp.einsum('tk,tif->kif', row_hot[group_index, slab_index], products)
            return lax.optimization_barrier(partial_value.astype(jnp.bfloat16)).astype(jnp.float32)

        partials = lax.map(one_group, jnp.arange(N_REP, dtype=jnp.int32))
        return jnp.sum(partials, axis=0).reshape(SLAB, F).astype(jnp.bfloat16)

    hidden = lax.map(forward_slab, jnp.arange(N_BLK, dtype=jnp.int32))
    hidden_rows = hidden.reshape(NODES, F)
    preact = jnp.dot(hidden_rows, weight, preferred_element_type=jnp.float32)
    gating = jax.nn.sigmoid(preact)
    layer_out = (preact * gating).astype(jnp.bfloat16).reshape(N_BLK, N_REP, XR, F)
    slope_term = gating * (1.0 + preact * (1.0 - gating))
    grad_pre = (cotangent.reshape(NODES, F).astype(jnp.float32) * slope_term).astype(jnp.bfloat16)
    grad_weight = jnp.dot(hidden_rows.T, grad_pre, preferred_element_type=jnp.float32)
    grad_hidden = jnp.dot(grad_pre, weight.T, preferred_element_type=jnp.float32).astype(jnp.bfloat16)
    grad_blocks = grad_hidden.reshape(N_BLK, SLAB_BLOCKS, TILE, F)

    def backward_group(group_index):
        def add_slab(total, slab_index):
            picked = jnp.take(grad_blocks[slab_index], tile_row[group_index, slab_index], axis=0)
            products = jnp.einsum('tij,tif->tjf', tile_values[group_index, slab_index].astype(jnp.float32), picked.astype(jnp.float32))
            partial_value = jnp.einsum('tk,tjf->kjf', col_hot[group_index, slab_index], products)
            partial_value = lax.optimization_barrier(partial_value.astype(jnp.bfloat16)).astype(jnp.float32)
            return total + partial_value, None

        total, unused = lax.scan(add_slab, jnp.zeros((GROUP_BLOCKS, TILE, F), jnp.float32), jnp.arange(N_BLK, dtype=jnp.int32))
        return total.reshape(GROUP, F).astype(jnp.bfloat16)

    grad_features = lax.map(backward_group, jnp.arange(N_REP, dtype=jnp.int32)).reshape(NODES, F)
    return (layer_out, grad_weight, grad_features)
```

```python
import functools

import jax
import jax.numpy as jnp
from jax import lax
from jax.experimental import pallas as pl
from jax.experimental.pallas import tpu as pltpu
from jax.sharding import PartitionSpec as P

MESH = pl.DeviceIdType.MESH
BF16, F32 = jnp.bfloat16, jnp.float32
PIECES = 1


def partner(index, step):
    out, bit = index, 1
    while bit <= step:
        if step & bit:
            out = out + bit * (1 - 2 * ((index // bit) % 2))
        bit *= 2
    return out


def kernel(
    n_rep, n_blk, pieces,
    slot_ref, tiles_hbm, x_hbm, w_hbm, cot_hbm,
    layer_ref, gw_ref, gf_ref,
    tiles, dense, xg, w, cot, acc, pout, pin, gg, bsib_out, bsib_in, bout, bin_, brelay,
    wsib_out, wsib_in, wl_out, wl_in, wr_in, wgath, wpart, fin,
    loc, xs, xr, ps, pr, gs, gr, bs, br_sib, br_line, br_relay, ws, wr,
):
    rows, feats = x_hbm.shape
    tile = tiles.shape[1]
    per = rows // tile
    line = n_blk // 2
    slab, group = rows * n_rep, rows * n_blk
    slab_blocks, group_blocks = slab // tile, group // tile
    fh = feats // pieces
    relay = line == 4
    r, b = lax.axis_index("rep"), lax.axis_index("blk")
    z, c = b // 2, b % 2
    other = b + 1 - 2 * c
    outer = jnp.logical_or(z == 0, z == line - 1)

    def blk_at(m):
        return partner(z, m) * 2 + c

    def remote(src, dst, send, recv, rep, blk):
        return pltpu.make_async_remote_copy(
            src_ref=src, dst_ref=dst, send_sem=send, recv_sem=recv,
            device_id={"rep": rep, "blk": blk}, device_id_type=MESH,
        )

    def arrive(dst, send, recv, rep, blk):
        remote(dst, dst, send, recv, rep, blk).wait_recv()

    fetch = [
        pltpu.make_async_copy(x_hbm, xg.at[b], loc.at[0]),
        pltpu.make_async_copy(tiles_hbm, tiles.at[pl.ds(1, tiles.shape[0] - 1)], loc.at[1]),
        pltpu.make_async_copy(w_hbm, w, loc.at[2]),
        pltpu.make_async_copy(cot_hbm, cot, loc.at[3]),
    ]
    for copy in fetch:
        copy.start()

    barrier = pltpu.get_barrier_semaphore()
    friends = [(r, blk_at(m)) for m in range(1, line)] + [(r, other)]
    friends += [(partner(r, m), b) for m in range(1, n_rep)]
    for rep, blk in friends:
        pl.semaphore_signal(
            barrier, inc=1, device_id={"rep": rep, "blk": blk}, device_id_type=MESH
        )
    tiles[0] = jnp.zeros((tile, tile), BF16)
    pl.semaphore_wait(barrier, len(friends))

    def cols(h):
        return pl.ds(h * fh, fh)

    sends = []

    def x_line(h, m):
        return remote(
            x_hbm.at[:, cols(h)], xg.at[b, :, cols(h)], xs.at[h, 0, m], xr.at[h, b], r, blk_at(m)
        )

    def x_relay(h):
        via = blk_at(2)
        return remote(
            xg.at[via, :, cols(h)], xg.at[via, :, cols(h)], xs.at[h, 0, 0], xr.at[h, via],
            r, blk_at(1),
        )

    def x_pass(h, m):
        blk = blk_at(m)
        src = x_hbm.at[:, cols(h)] if m == 0 else xg.at[blk, :, cols(h)]
        return remote(
            src, xg.at[blk, :, cols(h)], xs.at[h, 1, m], xr.at[h, blk], r, other
        )

    for h in range(pieces):
        for m in range(line - 1, 0, -1):
            if relay and m == 3:
                @pl.when(jnp.logical_not(outer))
                def _():
                    x_line(h, m).start()
            else:
                x_line(h, m).start()
        x_pass(h, 0).start()

    fetch[1].wait()

    def lay_out(n, carry):
        panel, k = n // slab_blocks, n % slab_blocks
        for j in range(per):
            slot = slot_ref[k * group_blocks + panel * per + j]
            start = pl.multiple_of(panel * slab + k * tile, tile)
            dense[pl.ds(start, tile), j * tile:(j + 1) * tile] = tiles[slot]
        return carry

    lax.fori_loop(0, n_blk * slab_blocks, lay_out, 0, unroll=4)
    fetch[0].wait()

    chunk = 4 * rows if slab % (4 * rows) == 0 else rows

    def add_panel(h, base, height, rhs, first):
        for at in range(0, height, chunk):
            lhs = dense[pl.ds(pl.multiple_of(base + at, tile), chunk), :]
            part = jnp.dot(lhs, rhs, preferred_element_type=F32)
            if first:
                acc[pl.ds(at, chunk), cols(h)] = part
            else:
                acc[pl.ds(at, chunk), cols(h)] += part

    def p_send(h, m):
        to = partner(r, m)
        return remote(
            pout.at[to, :, cols(h)], pin.at[r, :, cols(h)], ps.at[h, m], pr.at[h, r], to, b
        )

    for h in range(pieces):
        add_panel(h, b * slab, slab, xg[b, :, cols(h)], True)
        arrive(xg.at[other, :, cols(h)], xs.at[h, 1, 0], xr.at[h, other], r, other)
        add_panel(h, other * slab, slab, xg[other, :, cols(h)], False)
        for m in range(1, line):
            blk = blk_at(m)
            arrive(xg.at[blk, :, cols(h)], xs.at[h, 0, m], xr.at[h, blk], r, blk)
            if relay and m == 2:
                @pl.when(jnp.logical_not(outer))
                def _():
                    x_relay(h).start()
            x_pass(h, m).start()
            add_panel(h, blk * slab, slab, xg[blk, :, cols(h)], False)
            if m > 1:
                last = partner(z, m - 1) * 2 + 1 - c
                arrive(xg.at[last, :, cols(h)], xs.at[h, 1, m - 1], xr.at[h, last], r, other)
                add_panel(h, last * slab, slab, xg[last, :, cols(h)], False)
        last = partner(z, line - 1) * 2 + 1 - c
        arrive(xg.at[last, :, cols(h)], xs.at[h, 1, line - 1], xr.at[h, last], r, other)
        for m in range(n_rep - 1, -1, -1):
            to = partner(r, m)
            at = pl.multiple_of(to * rows, rows)
            panel = dense[pl.ds(pl.multiple_of(last * slab + to * rows, rows), rows), :]
            part = acc[pl.ds(at, rows), cols(h)] + jnp.dot(
                panel, xg[last, :, cols(h)], preferred_element_type=F32
            )
            pout[to, :, cols(h)] = part.astype(BF16)
            if m:
                p_send(h, m).start()

    def turn(t, carry):
        tiles[t] = tiles[t].T
        return carry

    lax.fori_loop(1, tiles.shape[0], turn, 0)

    def lay_out_turned(n, carry):
        panel, k = n // group_blocks, n % group_blocks
        for j in range(per):
            slot = slot_ref[(panel * per + j) * group_blocks + k]
            start = pl.multiple_of(panel * group + k * tile, tile)
            dense[pl.ds(start, tile), j * tile:(j + 1) * tile] = tiles[slot]
        return carry

    lax.fori_loop(0, n_rep * group_blocks, lay_out_turned, 0, unroll=4)
    fetch[2].wait()
    fetch[3].wait()

    total = pout[r].astype(F32)
    for m in range(1, n_rep):
        peer = partner(r, m)
        for h in range(pieces):
            arrive(pin.at[peer, :, cols(h)], ps.at[h, m], pr.at[h, peer], peer, b)
        total = total + pin[peer].astype(F32)
    hidden = total.astype(BF16)
    preact = jnp.dot(hidden, w[...], preferred_element_type=F32)
    gate = jax.nn.sigmoid(preact)
    slope = gate * (1.0 + preact * (1.0 - gate))
    grad_pre = (cot[...].astype(F32) * slope).astype(BF16)

    def g_send(h, m):
        to = partner(r, m)
        return remote(
            gg.at[r, :, cols(h)], gg.at[r, :, cols(h)], gs.at[h, m], gr.at[h, r], to, b
        )

    for h in range(pieces):
        gg[r, :, cols(h)] = lax.dot_general(
            grad_pre, w[cols(h), :], (((1,), (1,)), ((), ())), preferred_element_type=F32
        ).astype(BF16)
        for m in range(n_rep - 1, 0, -1):
            g_send(h, m).start()

    layer_ref[...] = (preact * gate).astype(BF16)
    wpart[...] = lax.dot_general(
        hidden, grad_pre, (((0,), (0,)), ((), ())), preferred_element_type=F32
    )
    half = feats // 2
    share = half // line
    kind = wl_out.dtype
    mine_at, other_at = c * half, (1 - c) * half
    wsib_out[...] = wpart[pl.ds(pl.multiple_of(other_at, half), half), :].astype(kind)
    w_sib = remote(wsib_out, wsib_in, ws.at[0, 0], wr.at[0, 0], r, other)
    w_sib.start()

    add_panel(0, r * group, group, gg[r, :, cols(0)], True)

    w_sib.wait_recv()
    both = wpart[pl.ds(pl.multiple_of(mine_at, half), half), :] + wsib_in[...].astype(F32)
    wpart[pl.ds(0, half), :] = both
    for m in range(line):
        at = pl.multiple_of(partner(z, m) * share, share)
        wl_out[m] = wpart[pl.ds(at, share), :].astype(kind)

    def w_line(m):
        return remote(wl_out.at[m], wl_in.at[m], ws.at[1, m], wr.at[1, m], r, blk_at(m))

    for m in range(1, line):
        w_line(m).start()

    def w_rep(m):
        return remote(
            wr_in.at[r], wr_in.at[r], ws.at[2, m], wr.at[2, r], partner(r, m), b
        )

    def w_sum_line():
        part = wl_out[0].astype(F32)
        for m in range(1, line):
            w_line(m).wait_recv()
            part = part + wl_in[m].astype(F32)
        wr_in[r] = part.astype(kind)
        for m in range(1, n_rep):
            w_rep(m).start()

    def w_back(m):
        return remote(
            wgath.at[c, z], wgath.at[c, z], ws.at[3, m], wr.at[3, z], r, blk_at(m)
        )

    def w_pass(m):
        place = partner(z, m)
        return remote(
            wgath.at[c, place], wgath.at[c, place], ws.at[4, m], wr.at[4, place], r, other
        )

    def w_sum_rep():
        for m in range(1, n_rep):
            peer = partner(r, m)
            arrive(wr_in.at[peer], ws.at[2, m], wr.at[2, peer], peer, b)
        part = wr_in[0].astype(F32)
        for i in range(1, n_rep):
            part = part + wr_in[i].astype(F32)
        wgath[c, z] = part.astype(kind)
        for m in range(1, line):
            w_back(m).start()
        w_pass(0).start()

    def b_sib(h, m):
        place = partner(z, m)
        return remote(
            bsib_out.at[place, :, cols(h)], bsib_in.at[place, :, cols(h)],
            bs.at[h, 0, m], br_sib.at[h, place], r, other,
        )

    def b_line(h, m):
        return remote(
            bout.at[m, :, cols(h)], bin_.at[m, :, cols(h)],
            bs.at[h, 1, m], br_line.at[h, m], r, blk_at(m),
        )

    def b_relay(h):
        return remote(
            bout.at[3, :, cols(h)], brelay.at[:, cols(h)],
            bs.at[h, 1, 3], br_relay.at[h], r, blk_at(2),
        )

    for h in range(pieces):
        if h:
            add_panel(h, r * group, group, gg[r, :, cols(h)], True)
        for m in range(1, n_rep):
            peer = partner(r, m)
            arrive(gg.at[peer, :, cols(h)], gs.at[h, m], gr.at[h, peer], peer, b)
            if m < n_rep - 1:
                add_panel(h, peer * group, group, gg[peer, :, cols(h)], False)
            if m == 1 and h == 0:
                w_sum_line()
        peer = partner(r, n_rep - 1)
        rhs = gg[peer, :, cols(h)]

        def finish(blk):
            at = pl.multiple_of(blk * rows, rows)
            panel = dense[pl.ds(pl.multiple_of(peer * group + blk * rows, rows), rows), :]
            return acc[pl.ds(at, rows), cols(h)] + jnp.dot(
                panel, rhs, preferred_element_type=F32
            )

        for m in range(line - 1, -1, -1):
            place = partner(z, m)
            bsib_out[place, :, cols(h)] = finish(place * 2 + 1 - c).astype(BF16)
            b_sib(h, m).start()
        if h == pieces - 1:
            w_sum_rep()
        for m in range(line - 1, -1, -1):
            place = partner(z, m)
            mine = finish(place * 2 + c)
            arrive(
                bsib_in.at[place, :, cols(h)], bs.at[h, 0, m], br_sib.at[h, place], r, other
            )
            mine = mine + bsib_in[place, :, cols(h)].astype(F32)
            if m == 0:
                fin[0, :, cols(h)] = mine
            elif relay and m == 3:
                bout[m, :, cols(h)] = mine.astype(BF16)

                @pl.when(outer)
                def _():
                    b_relay(h).start()

                @pl.when(jnp.logical_not(outer))
                def _():
                    b_line(h, m).start()
            elif relay and m == 1:
                fin[1, :, cols(h)] = mine

                @pl.when(jnp.logical_not(outer))
                def _():
                    b_relay(h).wait_recv()
                    fin[1, :, cols(h)] += brelay[:, cols(h)].astype(F32)

                bout[m, :, cols(h)] = fin[1, :, cols(h)].astype(BF16)
                b_line(h, m).start()
            else:
                bout[m, :, cols(h)] = mine.astype(BF16)
                b_line(h, m).start()

    for m in range(1, line):
        place = partner(z, m)
        arrive(wgath.at[c, place], ws.at[3, m], wr.at[3, place], r, blk_at(m))
        w_pass(m).start()

    for h in range(pieces):
        for m in range(1, line):
            if relay and m == 3:
                @pl.when(jnp.logical_not(outer))
                def _():
                    b_line(h, m).wait_recv()
                    fin[0, :, cols(h)] += bin_[m, :, cols(h)].astype(F32)
            else:
                b_line(h, m).wait_recv()
                fin[0, :, cols(h)] += bin_[m, :, cols(h)].astype(F32)
    gf_ref[...] = fin[0].astype(BF16)

    for m in range(line):
        place = partner(z, m)
        arrive(wgath.at[1 - c, place], ws.at[4, m], wr.at[4, place], r, other)
    for core in range(2):
        for place in range(line):
            at = core * half + place * share
            gw_ref[at:at + share, :] = wgath[core, place].astype(F32)

    for h in range(pieces):
        for m in range(1, line):
            if relay and m == 3:
                @pl.when(jnp.logical_not(outer))
                def _():
                    x_line(h, m).wait_send()
                    x_relay(h).wait_send()
            else:
                x_line(h, m).wait_send()
            b_line(h, m).wait_send()
        for m in range(line):
            x_pass(h, m).wait_send()
            b_sib(h, m).wait_send()
        for m in range(1, n_rep):
            p_send(h, m).wait_send()
            g_send(h, m).wait_send()
    w_sib.wait_send()
    for m in range(1, line):
        w_line(m).wait_send()
        w_back(m).wait_send()
    for m in range(line):
        w_pass(m).wait_send()
    for m in range(1, n_rep):
        w_rep(m).wait_send()


def on_device(n_rep, n_blk, node_features, tile_values, tile_row, tile_col, tile_count, weight, cotangent):
    rows, feats = node_features.shape
    slots, tile = tile_values.shape[2], tile_values.shape[3]
    slab_blocks = n_rep * rows // tile
    group_blocks = n_blk * rows // tile
    line = n_blk // 2
    share = feats // 2 // line
    kind = BF16 if share % 16 == 0 else F32
    number = jnp.arange(slots, dtype=jnp.int32)
    place = jnp.where(number < tile_count[0, 0], tile_row[0, 0] * group_blocks + tile_col[0, 0], -1)
    spots = jnp.arange(slab_blocks * group_blocks, dtype=jnp.int32)
    slot_of = jnp.max(
        jnp.where(place[:, None] == spots[None, :], number[:, None] + 1, 0), axis=0
    )
    block = (rows, feats)
    h = PIECES
    dma = pltpu.SemaphoreType.DMA
    layer, gw, gf = pl.pallas_call(
        functools.partial(kernel, n_rep, n_blk, h),
        out_shape=(
            jax.ShapeDtypeStruct(block, BF16),
            jax.ShapeDtypeStruct((feats, feats), F32),
            jax.ShapeDtypeStruct(block, BF16),
        ),
        in_specs=[pl.BlockSpec(memory_space=pltpu.SMEM)] + [pl.BlockSpec(memory_space=pl.ANY)] * 4,
        out_specs=tuple([pl.BlockSpec(memory_space=pltpu.VMEM)] * 3),
        scratch_shapes=[
            pltpu.VMEM((slots + 1, tile, tile), BF16),
            pltpu.VMEM((n_blk * n_rep * rows, rows), BF16),
            pltpu.VMEM((n_blk,) + block, BF16),
            pltpu.VMEM((feats, feats), BF16),
            pltpu.VMEM(block, BF16),
            pltpu.VMEM((max(n_blk, n_rep) * rows, feats), F32),
            pltpu.VMEM((n_rep,) + block, BF16),
            pltpu.VMEM((n_rep,) + block, BF16),
            pltpu.VMEM((n_rep,) + block, BF16),
            pltpu.VMEM((line,) + block, BF16),
            pltpu.VMEM((line,) + block, BF16),
            pltpu.VMEM((line,) + block, BF16),
            pltpu.VMEM((line,) + block, BF16),
            pltpu.VMEM(block, BF16),
            pltpu.VMEM((feats // 2, feats), kind),
            pltpu.VMEM((feats // 2, feats), kind),
            pltpu.VMEM((line, share, feats), kind),
            pltpu.VMEM((line, share, feats), kind),
            pltpu.VMEM((n_rep, share, feats), kind),
            pltpu.VMEM((2, line, share, feats), kind),
            pltpu.VMEM((feats, feats), F32),
            pltpu.VMEM((2,) + block, F32),
            dma((4,)),
            dma((h, 2, line)),
            dma((h, n_blk)),
            dma((h, n_rep)),
            dma((h, n_rep)),
            dma((h, n_rep)),
            dma((h, n_rep)),
            dma((h, 2, line)),
            dma((h, line)),
            dma((h, line)),
            dma((h,)),
            dma((5, max(line, n_rep))),
            dma((5, max(line, n_rep))),
        ],
        compiler_params=pltpu.CompilerParams(
            collective_id=0, has_side_effects=True, vmem_limit_bytes=62 * 1024 * 1024
        ),
    )(slot_of, tile_values[0, 0], node_features, weight, cotangent[0, 0])
    return layer.reshape((1, 1) + block), gw, gf


def solution(mesh):
    placed = (
        P(("rep", "blk"), None),
        P("rep", "blk", None, None, None),
        P("rep", "blk", None),
        P("rep", "blk", None),
        P("rep", "blk"),
        P(),
        P("blk", "rep", None, None),
    )
    return jax.shard_map(
        functools.partial(on_device, mesh.shape["rep"], mesh.shape["blk"]),
        mesh=mesh,
        in_specs=placed,
        out_specs=(P("blk", "rep", None, None), P(), P(("rep", "blk"), None)),
        check_vma=False,
    )
```

```python
import functools

import jax
import jax.numpy as jnp
from jax import lax
from jax.experimental import pallas as pl
from jax.experimental.pallas import tpu as pltpu
from jax.sharding import PartitionSpec as P

MESH = pl.DeviceIdType.MESH
BF16, F32 = jnp.bfloat16, jnp.float32
PIECES = 2


def partner(index, step):
    out, bit = index, 1
    while bit <= step:
        if step & bit:
            out = out + bit * (1 - 2 * ((index // bit) % 2))
        bit *= 2
    return out


def kernel(
    n_rep, n_blk, pieces,
    slot_ref, tiles_hbm, x_hbm, w_hbm, cot_hbm,
    layer_ref, gw_ref, gf_ref,
    tiles, dense, xg, w, cot, acc, pout, pin, gg, bsib_out, bsib_in, bout, bin_, brelay,
    wsib_out, wsib_in, wl_out, wl_in, wr_in, wgath, wpart, fin,
    loc, xs, xr, ps, pr, gs, gr, bs, br_sib, br_line, br_relay, ws, wr,
):
    rows, feats = x_hbm.shape
    tile = tiles.shape[1]
    per = rows // tile
    line = n_blk // 2
    slab, group = rows * n_rep, rows * n_blk
    slab_blocks, group_blocks = slab // tile, group // tile
    fh = feats // pieces
    relay = line == 4
    r, b = lax.axis_index("rep"), lax.axis_index("blk")
    z, c = b // 2, b % 2
    other = b + 1 - 2 * c
    outer = jnp.logical_or(z == 0, z == line - 1)

    def blk_at(m):
        return partner(z, m) * 2 + c

    def remote(src, dst, send, recv, rep, blk):
        return pltpu.make_async_remote_copy(
            src_ref=src, dst_ref=dst, send_sem=send, recv_sem=recv,
            device_id={"rep": rep, "blk": blk}, device_id_type=MESH,
        )

    def arrive(dst, send, recv, rep, blk):
        remote(dst, dst, send, recv, rep, blk).wait_recv()

    fetch = [
        pltpu.make_async_copy(x_hbm, xg.at[b], loc.at[0]),
        pltpu.make_async_copy(tiles_hbm, tiles.at[pl.ds(1, tiles.shape[0] - 1)], loc.at[1]),
        pltpu.make_async_copy(w_hbm, w, loc.at[2]),
        pltpu.make_async_copy(cot_hbm, cot, loc.at[3]),
    ]
    for copy in fetch:
        copy.start()

    barrier = pltpu.get_barrier_semaphore()
    friends = [(r, blk_at(m)) for m in range(1, line)] + [(r, other)]
    friends += [(partner(r, m), b) for m in range(1, n_rep)]
    for rep, blk in friends:
        pl.semaphore_signal(
            barrier, inc=1, device_id={"rep": rep, "blk": blk}, device_id_type=MESH
        )
    tiles[0] = jnp.zeros((tile, tile), BF16)
    pl.semaphore_wait(barrier, len(friends))

    def cols(h):
        return pl.ds(h * fh, fh)

    sends = []

    def x_line(h, m):
        return remote(
            x_hbm.at[:, cols(h)], xg.at[b, :, cols(h)], xs.at[h, 0, m], xr.at[h, b], r, blk_at(m)
        )

    def x_relay(h):
        via = blk_at(2)
        return remote(
            xg.at[via, :, cols(h)], xg.at[via, :, cols(h)], xs.at[h, 0, 0], xr.at[h, via],
            r, blk_at(1),
        )

    def x_pass(h, m):
        blk = blk_at(m)
        src = x_hbm.at[:, cols(h)] if m == 0 else xg.at[blk, :, cols(h)]
        return remote(
            src, xg.at[blk, :, cols(h)], xs.at[h, 1, m], xr.at[h, blk], r, other
        )

    for h in range(pieces):
        for m in range(line - 1, 0, -1):
            if relay and m == 3:
                @pl.when(jnp.logical_not(outer))
                def _():
                    x_line(h, m).start()
            else:
                x_line(h, m).start()
        x_pass(h, 0).start()

    fetch[1].wait()

    def lay_out(n, carry):
        panel, k = n // slab_blocks, n % slab_blocks
        for j in range(per):
            slot = slot_ref[k * group_blocks + panel * per + j]
            start = pl.multiple_of(panel * slab + k * tile, tile)
            dense[pl.ds(start, tile), j * tile:(j + 1) * tile] = tiles[slot]
        return carry

    lax.fori_loop(0, n_blk * slab_blocks, lay_out, 0, unroll=4)
    fetch[0].wait()

    chunk = 4 * rows if slab % (4 * rows) == 0 else rows

    def add_panel(h, base, height, rhs, first):
        for at in range(0, height, chunk):
            lhs = dense[pl.ds(pl.multiple_of(base + at, tile), chunk), :]
            part = jnp.dot(lhs, rhs, preferred_element_type=F32)
            if first:
                acc[pl.ds(at, chunk), cols(h)] = part
            else:
                acc[pl.ds(at, chunk), cols(h)] += part

    def p_send(h, m):
        to = partner(r, m)
        return remote(
            pout.at[to, :, cols(h)], pin.at[r, :, cols(h)], ps.at[h, m], pr.at[h, r], to, b
        )

    for h in range(pieces):
        add_panel(h, b * slab, slab, xg[b, :, cols(h)], True)
        arrive(xg.at[other, :, cols(h)], xs.at[h, 1, 0], xr.at[h, other], r, other)
        add_panel(h, other * slab, slab, xg[other, :, cols(h)], False)
        for m in range(1, line):
            blk = blk_at(m)
            arrive(xg.at[blk, :, cols(h)], xs.at[h, 0, m], xr.at[h, blk], r, blk)
            if relay and m == 2:
                @pl.when(jnp.logical_not(outer))
                def _():
                    x_relay(h).start()
            x_pass(h, m).start()
            add_panel(h, blk * slab, slab, xg[blk, :, cols(h)], False)
            if m > 1:
                last = partner(z, m - 1) * 2 + 1 - c
                arrive(xg.at[last, :, cols(h)], xs.at[h, 1, m - 1], xr.at[h, last], r, other)
                add_panel(h, last * slab, slab, xg[last, :, cols(h)], False)
        last = partner(z, line - 1) * 2 + 1 - c
        arrive(xg.at[last, :, cols(h)], xs.at[h, 1, line - 1], xr.at[h, last], r, other)
        for m in range(n_rep - 1, -1, -1):
            to = partner(r, m)
            at = pl.multiple_of(to * rows, rows)
            panel = dense[pl.ds(pl.multiple_of(last * slab + to * rows, rows), rows), :]
            part = acc[pl.ds(at, rows), cols(h)] + jnp.dot(
                panel, xg[last, :, cols(h)], preferred_element_type=F32
            )
            pout[to, :, cols(h)] = part.astype(BF16)
            if m:
                p_send(h, m).start()

    def turn(t, carry):
        tiles[t] = tiles[t].T
        return carry

    lax.fori_loop(1, tiles.shape[0], turn, 0)

    def lay_out_turned(n, carry):
        panel, k = n // group_blocks, n % group_blocks
        for j in range(per):
            slot = slot_ref[(panel * per + j) * group_blocks + k]
            start = pl.multiple_of(panel * group + k * tile, tile)
            dense[pl.ds(start, tile), j * tile:(j + 1) * tile] = tiles[slot]
        return carry

    lax.fori_loop(0, n_rep * group_blocks, lay_out_turned, 0, unroll=4)
    fetch[2].wait()
    fetch[3].wait()

    total = pout[r].astype(F32)
    for m in range(1, n_rep):
        peer = partner(r, m)
        for h in range(pieces):
            arrive(pin.at[peer, :, cols(h)], ps.at[h, m], pr.at[h, peer], peer, b)
        total = total + pin[peer].astype(F32)
    hidden = total.astype(BF16)
    preact = jnp.dot(hidden, w[...], preferred_element_type=F32)
    gate = jax.nn.sigmoid(preact)
    slope = gate * (1.0 + preact * (1.0 - gate))
    grad_pre = (cot[...].astype(F32) * slope).astype(BF16)

    def g_send(h, m):
        to = partner(r, m)
        return remote(
            gg.at[r, :, cols(h)], gg.at[r, :, cols(h)], gs.at[h, m], gr.at[h, r], to, b
        )

    for h in range(pieces):
        gg[r, :, cols(h)] = lax.dot_general(
            grad_pre, w[cols(h), :], (((1,), (1,)), ((), ())), preferred_element_type=F32
        ).astype(BF16)
        for m in range(n_rep - 1, 0, -1):
            g_send(h, m).start()

    layer_ref[...] = (preact * gate).astype(BF16)
    wpart[...] = lax.dot_general(
        hidden, grad_pre, (((0,), (0,)), ((), ())), preferred_element_type=F32
    )
    half = feats // 2
    share = half // line
    kind = wl_out.dtype
    mine_at, other_at = c * half, (1 - c) * half
    wsib_out[...] = wpart[pl.ds(pl.multiple_of(other_at, half), half), :].astype(kind)
    w_sib = remote(wsib_out, wsib_in, ws.at[0, 0], wr.at[0, 0], r, other)
    w_sib.start()

    add_panel(0, r * group, group, gg[r, :, cols(0)], True)

    w_sib.wait_recv()
    both = wpart[pl.ds(pl.multiple_of(mine_at, half), half), :] + wsib_in[...].astype(F32)
    wpart[pl.ds(0, half), :] = both
    for m in range(line):
        at = pl.multiple_of(partner(z, m) * share, share)
        wl_out[m] = wpart[pl.ds(at, share), :].astype(kind)

    def w_line(m):
        return remote(wl_out.at[m], wl_in.at[m], ws.at[1, m], wr.at[1, m], r, blk_at(m))

    for m in range(1, line):
        w_line(m).start()

    def w_rep(m):
        return remote(
            wr_in.at[r], wr_in.at[r], ws.at[2, m], wr.at[2, r], partner(r, m), b
        )

    def w_sum_line():
        part = wl_out[0].astype(F32)
        for m in range(1, line):
            w_line(m).wait_recv()
            part = part + wl_in[m].astype(F32)
        wr_in[r] = part.astype(kind)
        for m in range(1, n_rep):
            w_rep(m).start()

    def w_back(m):
        return remote(
            wgath.at[c, z], wgath.at[c, z], ws.at[3, m], wr.at[3, z], r, blk_at(m)
        )

    def w_pass(m):
        place = partner(z, m)
        return remote(
            wgath.at[c, place], wgath.at[c, place], ws.at[4, m], wr.at[4, place], r, other
        )

    def w_sum_rep():
        for m in range(1, n_rep):
            peer = partner(r, m)
            arrive(wr_in.at[peer], ws.at[2, m], wr.at[2, peer], peer, b)
        part = wr_in[0].astype(F32)
        for i in range(1, n_rep):
            part = part + wr_in[i].astype(F32)
        wgath[c, z] = part.astype(kind)
        for m in range(1, line):
            w_back(m).start()
        w_pass(0).start()

    def b_sib(h, m):
        place = partner(z, m)
        return remote(
            bsib_out.at[place, :, cols(h)], bsib_in.at[place, :, cols(h)],
            bs.at[h, 0, m], br_sib.at[h, place], r, other,
        )

    def b_line(h, m):
        return remote(
            bout.at[m, :, cols(h)], bin_.at[m, :, cols(h)],
            bs.at[h, 1, m], br_line.at[h, m], r, blk_at(m),
        )

    def b_relay(h):
        return remote(
            bout.at[3, :, cols(h)], brelay.at[:, cols(h)],
            bs.at[h, 1, 3], br_relay.at[h], r, blk_at(2),
        )

    for h in range(pieces):
        if h:
            add_panel(h, r * group, group, gg[r, :, cols(h)], True)
        for m in range(1, n_rep):
            peer = partner(r, m)
            arrive(gg.at[peer, :, cols(h)], gs.at[h, m], gr.at[h, peer], peer, b)
            if m < n_rep - 1:
                add_panel(h, peer * group, group, gg[peer, :, cols(h)], False)
            if m == 1 and h == 0:
                w_sum_line()
        peer = partner(r, n_rep - 1)
        rhs = gg[peer, :, cols(h)]

        def finish(blk):
            at = pl.multiple_of(blk * rows, rows)
            panel = dense[pl.ds(pl.multiple_of(peer * group + blk * rows, rows), rows), :]
            return acc[pl.ds(at, rows), cols(h)] + jnp.dot(
                panel, rhs, preferred_element_type=F32
            )

        for m in range(line - 1, -1, -1):
            place = partner(z, m)
            bsib_out[place, :, cols(h)] = finish(place * 2 + 1 - c).astype(BF16)
            b_sib(h, m).start()
        if h == pieces - 1:
            w_sum_rep()
        for m in range(line - 1, -1, -1):
            place = partner(z, m)
            mine = finish(place * 2 + c)
            arrive(
                bsib_in.at[place, :, cols(h)], bs.at[h, 0, m], br_sib.at[h, place], r, other
            )
            mine = mine + bsib_in[place, :, cols(h)].astype(F32)
            if m == 0:
                fin[0, :, cols(h)] = mine
            elif relay and m == 3:
                bout[m, :, cols(h)] = mine.astype(BF16)

                @pl.when(outer)
                def _():
                    b_relay(h).start()

                @pl.when(jnp.logical_not(outer))
                def _():
                    b_line(h, m).start()
            elif relay and m == 1:
                fin[1, :, cols(h)] = mine

                @pl.when(jnp.logical_not(outer))
                def _():
                    b_relay(h).wait_recv()
                    fin[1, :, cols(h)] += brelay[:, cols(h)].astype(F32)

                bout[m, :, cols(h)] = fin[1, :, cols(h)].astype(BF16)
                b_line(h, m).start()
            else:
                bout[m, :, cols(h)] = mine.astype(BF16)
                b_line(h, m).start()

    for m in range(1, line):
        place = partner(z, m)
        arrive(wgath.at[c, place], ws.at[3, m], wr.at[3, place], r, blk_at(m))
        w_pass(m).start()

    for h in range(pieces):
        for m in range(1, line):
            if relay and m == 3:
                @pl.when(jnp.logical_not(outer))
                def _():
                    b_line(h, m).wait_recv()
                    fin[0, :, cols(h)] += bin_[m, :, cols(h)].astype(F32)
            else:
                b_line(h, m).wait_recv()
                fin[0, :, cols(h)] += bin_[m, :, cols(h)].astype(F32)
    gf_ref[...] = fin[0].astype(BF16)

    for m in range(line):
        place = partner(z, m)
        arrive(wgath.at[1 - c, place], ws.at[4, m], wr.at[4, place], r, other)
    for core in range(2):
        for place in range(line):
            at = core * half + place * share
            gw_ref[at:at + share, :] = wgath[core, place].astype(F32)

    for h in range(pieces):
        for m in range(1, line):
            if relay and m == 3:
                @pl.when(jnp.logical_not(outer))
                def _():
                    x_line(h, m).wait_send()
                    x_relay(h).wait_send()
            else:
                x_line(h, m).wait_send()
            b_line(h, m).wait_send()
        for m in range(line):
            x_pass(h, m).wait_send()
            b_sib(h, m).wait_send()
        for m in range(1, n_rep):
            p_send(h, m).wait_send()
            g_send(h, m).wait_send()
    w_sib.wait_send()
    for m in range(1, line):
        w_line(m).wait_send()
        w_back(m).wait_send()
    for m in range(line):
        w_pass(m).wait_send()
    for m in range(1, n_rep):
        w_rep(m).wait_send()


def on_device(n_rep, n_blk, node_features, tile_values, tile_row, tile_col, tile_count, weight, cotangent):
    rows, feats = node_features.shape
    slots, tile = tile_values.shape[2], tile_values.shape[3]
    slab_blocks = n_rep * rows // tile
    group_blocks = n_blk * rows // tile
    line = n_blk // 2
    share = feats // 2 // line
    kind = BF16 if share % 16 == 0 else F32
    number = jnp.arange(slots, dtype=jnp.int32)
    place = jnp.where(number < tile_count[0, 0], tile_row[0, 0] * group_blocks + tile_col[0, 0], -1)
    spots = jnp.arange(slab_blocks * group_blocks, dtype=jnp.int32)
    slot_of = jnp.max(
        jnp.where(place[:, None] == spots[None, :], number[:, None] + 1, 0), axis=0
    )
    block = (rows, feats)
    h = PIECES
    dma = pltpu.SemaphoreType.DMA
    layer, gw, gf = pl.pallas_call(
        functools.partial(kernel, n_rep, n_blk, h),
        out_shape=(
            jax.ShapeDtypeStruct(block, BF16),
            jax.ShapeDtypeStruct((feats, feats), F32),
            jax.ShapeDtypeStruct(block, BF16),
        ),
        in_specs=[pl.BlockSpec(memory_space=pltpu.SMEM)] + [pl.BlockSpec(memory_space=pl.ANY)] * 4,
        out_specs=tuple([pl.BlockSpec(memory_space=pltpu.VMEM)] * 3),
        scratch_shapes=[
            pltpu.VMEM((slots + 1, tile, tile), BF16),
            pltpu.VMEM((n_blk * n_rep * rows, rows), BF16),
            pltpu.VMEM((n_blk,) + block, BF16),
            pltpu.VMEM((feats, feats), BF16),
            pltpu.VMEM(block, BF16),
            pltpu.VMEM((max(n_blk, n_rep) * rows, feats), F32),
            pltpu.VMEM((n_rep,) + block, BF16),
            pltpu.VMEM((n_rep,) + block, BF16),
            pltpu.VMEM((n_rep,) + block, BF16),
            pltpu.VMEM((line,) + block, BF16),
            pltpu.VMEM((line,) + block, BF16),
            pltpu.VMEM((line,) + block, BF16),
            pltpu.VMEM((line,) + block, BF16),
            pltpu.VMEM(block, BF16),
            pltpu.VMEM((feats // 2, feats), kind),
            pltpu.VMEM((feats // 2, feats), kind),
            pltpu.VMEM((line, share, feats), kind),
            pltpu.VMEM((line, share, feats), kind),
            pltpu.VMEM((n_rep, share, feats), kind),
            pltpu.VMEM((2, line, share, feats), kind),
            pltpu.VMEM((feats, feats), F32),
            pltpu.VMEM((2,) + block, F32),
            dma((4,)),
            dma((h, 2, line)),
            dma((h, n_blk)),
            dma((h, n_rep)),
            dma((h, n_rep)),
            dma((h, n_rep)),
            dma((h, n_rep)),
            dma((h, 2, line)),
            dma((h, line)),
            dma((h, line)),
            dma((h,)),
            dma((5, max(line, n_rep))),
            dma((5, max(line, n_rep))),
        ],
        compiler_params=pltpu.CompilerParams(
            collective_id=0, has_side_effects=True, vmem_limit_bytes=62 * 1024 * 1024
        ),
    )(slot_of, tile_values[0, 0], node_features, weight, cotangent[0, 0])
    return layer.reshape((1, 1) + block), gw, gf


def solution(mesh):
    placed = (
        P(("rep", "blk"), None),
        P("rep", "blk", None, None, None),
        P("rep", "blk", None),
        P("rep", "blk", None),
        P("rep", "blk"),
        P(),
        P("blk", "rep", None, None),
    )
    return jax.shard_map(
        functools.partial(on_device, mesh.shape["rep"], mesh.shape["blk"]),
        mesh=mesh,
        in_specs=placed,
        out_specs=(P("blk", "rep", None, None), P(), P(("rep", "blk"), None)),
        check_vma=False,
    )
```

```python
import functools

import jax
import jax.numpy as jnp
from jax import lax
from jax.experimental import pallas as pl
from jax.experimental.pallas import tpu as pltpu
from jax.sharding import PartitionSpec as P

MESH = pl.DeviceIdType.MESH
BF16, F32 = jnp.bfloat16, jnp.float32
PIECES = 2


def partner(index, step):
    out, bit = index, 1
    while bit <= step:
        if step & bit:
            out = out + bit * (1 - 2 * ((index // bit) % 2))
        bit *= 2
    return out


def kernel(
    n_rep, n_blk, pieces,
    row_ref, col_ref, count_ref, tiles_hbm, x_hbm, w_hbm, cot_hbm,
    layer_hbm, gw_hbm, gf_hbm,
    slot_vec, slot_ref, layer_ref, gw_ref, gf_ref,
    tiles, dense, xg, w, cot, acc, pout, pin, gg, bsib_out, bsib_in, bout, bin_, brelay,
    wsib_out, wsib_in, wl_out, wl_in, wr_in, wgath, wpart, fin,
    loc, xs, xr, ps, pr, gs, gr, bs, br_sib, br_line, br_relay, ws, wr,
):
    rows, feats = x_hbm.shape
    tile = tiles.shape[1]
    per = rows // tile
    line = n_blk // 2
    slab, group = rows * n_rep, rows * n_blk
    slab_blocks, group_blocks = slab // tile, group // tile
    fh = feats // pieces
    relay = line == 4
    r, b = lax.axis_index("rep"), lax.axis_index("blk")
    z, c = b // 2, b % 2
    other = b + 1 - 2 * c
    outer = jnp.logical_or(z == 0, z == line - 1)

    def blk_at(m):
        return partner(z, m) * 2 + c

    def remote(src, dst, send, recv, rep, blk):
        return pltpu.make_async_remote_copy(
            src_ref=src, dst_ref=dst, send_sem=send, recv_sem=recv,
            device_id={"rep": rep, "blk": blk}, device_id_type=MESH,
        )

    def arrive(dst, send, recv, rep, blk):
        remote(dst, dst, send, recv, rep, blk).wait_recv()

    fetch = [
        pltpu.make_async_copy(x_hbm, xg.at[b], loc.at[0]),
        pltpu.make_async_copy(tiles_hbm, tiles.at[pl.ds(1, tiles.shape[0] - 1)], loc.at[1]),
        pltpu.make_async_copy(w_hbm, w, loc.at[2]),
        pltpu.make_async_copy(cot_hbm, cot, loc.at[3]),
    ]
    for copy in fetch:
        copy.start()

    barrier = pltpu.get_barrier_semaphore()
    friends = [(r, blk_at(m)) for m in range(1, line)] + [(r, other)]
    friends += [(partner(r, m), b) for m in range(1, n_rep)]
    for rep, blk in friends:
        pl.semaphore_signal(
            barrier, inc=1, device_id={"rep": rep, "blk": blk}, device_id_type=MESH
        )
    tiles[0] = jnp.zeros((tile, tile), BF16)

    shape = slot_vec.shape
    spots = lax.broadcasted_iota(jnp.int32, shape, 0) * shape[1] + lax.broadcasted_iota(
        jnp.int32, shape, 1
    )

    def mark(t, found):
        named = jnp.where(t < count_ref[0, 0], row_ref[t] * group_blocks + col_ref[t], -1)
        return jnp.where(spots == named, t + 1, found)

    slot_vec[...] = lax.fori_loop(
        0, row_ref.shape[0], mark, jnp.zeros(shape, jnp.int32), unroll=8
    )
    slots_in = pltpu.make_async_copy(slot_vec, slot_ref, loc.at[4])
    slots_in.start()
    pl.semaphore_wait(barrier, len(friends))

    def cols(h):
        return pl.ds(h * fh, fh)

    sends = []

    def x_line(h, m):
        return remote(
            x_hbm.at[:, cols(h)], xg.at[b, :, cols(h)], xs.at[h, 0, m], xr.at[h, b], r, blk_at(m)
        )

    def x_relay(h):
        via = blk_at(2)
        return remote(
            xg.at[via, :, cols(h)], xg.at[via, :, cols(h)], xs.at[h, 0, 0], xr.at[h, via],
            r, blk_at(1),
        )

    def x_pass(h, m):
        blk = blk_at(m)
        src = x_hbm.at[:, cols(h)] if m == 0 else xg.at[blk, :, cols(h)]
        return remote(
            src, xg.at[blk, :, cols(h)], xs.at[h, 1, m], xr.at[h, blk], r, other
        )

    for h in range(pieces):
        for m in range(line - 1, 0, -1):
            if relay and m == 3:
                @pl.when(jnp.logical_not(outer))
                def _():
                    x_line(h, m).start()
            else:
                x_line(h, m).start()
        x_pass(h, 0).start()

    fetch[1].wait()
    slots_in.wait()

    def slot_at(pair):
        return slot_ref[pair // shape[1], pair % shape[1]]

    def lay_out(n, carry):
        panel, k = n // slab_blocks, n % slab_blocks
        for j in range(per):
            slot = slot_at(k * group_blocks + panel * per + j)
            start = pl.multiple_of(panel * slab + k * tile, tile)
            dense[pl.ds(start, tile), j * tile:(j + 1) * tile] = tiles[slot]
        return carry

    lax.fori_loop(0, n_blk * slab_blocks, lay_out, 0, unroll=4)
    fetch[0].wait()

    chunk = 4 * rows if slab % (4 * rows) == 0 else rows

    def add_panel(h, base, height, rhs, first):
        for at in range(0, height, chunk):
            lhs = dense[pl.ds(pl.multiple_of(base + at, tile), chunk), :]
            part = jnp.dot(lhs, rhs, preferred_element_type=F32)
            if first:
                acc[pl.ds(at, chunk), cols(h)] = part
            else:
                acc[pl.ds(at, chunk), cols(h)] += part

    def p_send(h, m):
        to = partner(r, m)
        return remote(
            pout.at[to, :, cols(h)], pin.at[r, :, cols(h)], ps.at[h, m], pr.at[h, r], to, b
        )

    for h in range(pieces):
        add_panel(h, b * slab, slab, xg[b, :, cols(h)], True)
        arrive(xg.at[other, :, cols(h)], xs.at[h, 1, 0], xr.at[h, other], r, other)
        add_panel(h, other * slab, slab, xg[other, :, cols(h)], False)
        for m in range(1, line):
            blk = blk_at(m)
            arrive(xg.at[blk, :, cols(h)], xs.at[h, 0, m], xr.at[h, blk], r, blk)
            if relay and m == 2:
                @pl.when(jnp.logical_not(outer))
                def _():
                    x_relay(h).start()
            x_pass(h, m).start()
            add_panel(h, blk * slab, slab, xg[blk, :, cols(h)], False)
            if m > 1:
                last = partner(z, m - 1) * 2 + 1 - c
                arrive(xg.at[last, :, cols(h)], xs.at[h, 1, m - 1], xr.at[h, last], r, other)
                add_panel(h, last * slab, slab, xg[last, :, cols(h)], False)
        last = partner(z, line - 1) * 2 + 1 - c
        arrive(xg.at[last, :, cols(h)], xs.at[h, 1, line - 1], xr.at[h, last], r, other)
        for m in range(n_rep - 1, -1, -1):
            to = partner(r, m)
            at = pl.multiple_of(to * rows, rows)
            panel = dense[pl.ds(pl.multiple_of(last * slab + to * rows, rows), rows), :]
            part = acc[pl.ds(at, rows), cols(h)] + jnp.dot(
                panel, xg[last, :, cols(h)], preferred_element_type=F32
            )
            pout[to, :, cols(h)] = part.astype(BF16)
            if m:
                p_send(h, m).start()

    def turn(t, carry):
        tiles[t] = tiles[t].T
        return carry

    lax.fori_loop(1, tiles.shape[0], turn, 0)

    def lay_out_turned(n, carry):
        panel, k = n // group_blocks, n % group_blocks
        for j in range(per):
            slot = slot_at((panel * per + j) * group_blocks + k)
            start = pl.multiple_of(panel * group + k * tile, tile)
            dense[pl.ds(start, tile), j * tile:(j + 1) * tile] = tiles[slot]
        return carry

    lax.fori_loop(0, n_rep * group_blocks, lay_out_turned, 0, unroll=4)
    fetch[2].wait()
    fetch[3].wait()

    total = pout[r].astype(F32)
    for m in range(1, n_rep):
        peer = partner(r, m)
        for h in range(pieces):
            arrive(pin.at[peer, :, cols(h)], ps.at[h, m], pr.at[h, peer], peer, b)
        total = total + pin[peer].astype(F32)
    hidden = total.astype(BF16)
    preact = jnp.dot(hidden, w[...], preferred_element_type=F32)
    gate = jax.nn.sigmoid(preact)
    slope = gate * (1.0 + preact * (1.0 - gate))
    grad_pre = (cot[...].astype(F32) * slope).astype(BF16)

    def g_send(h, m):
        to = partner(r, m)
        return remote(
            gg.at[r, :, cols(h)], gg.at[r, :, cols(h)], gs.at[h, m], gr.at[h, r], to, b
        )

    for h in range(pieces):
        gg[r, :, cols(h)] = lax.dot_general(
            grad_pre, w[cols(h), :], (((1,), (1,)), ((), ())), preferred_element_type=F32
        ).astype(BF16)
        for m in range(n_rep - 1, 0, -1):
            g_send(h, m).start()

    layer_ref[...] = (preact * gate).astype(BF16)
    layer_out = pltpu.make_async_copy(layer_ref, layer_hbm, loc.at[5])
    layer_out.start()
    wpart[...] = lax.dot_general(
        hidden, grad_pre, (((0,), (0,)), ((), ())), preferred_element_type=F32
    )
    half = feats // 2
    share = half // line
    kind = wl_out.dtype
    mine_at, other_at = c * half, (1 - c) * half
    wsib_out[...] = wpart[pl.ds(pl.multiple_of(other_at, half), half), :].astype(kind)
    w_sib = remote(wsib_out, wsib_in, ws.at[0, 0], wr.at[0, 0], r, other)
    w_sib.start()

    add_panel(0, r * group, group, gg[r, :, cols(0)], True)

    w_sib.wait_recv()
    both = wpart[pl.ds(pl.multiple_of(mine_at, half), half), :] + wsib_in[...].astype(F32)
    wpart[pl.ds(0, half), :] = both
    for m in range(line):
        at = pl.multiple_of(partner(z, m) * share, share)
        wl_out[m] = wpart[pl.ds(at, share), :].astype(kind)

    def w_line(m):
        return remote(wl_out.at[m], wl_in.at[m], ws.at[1, m], wr.at[1, m], r, blk_at(m))

    for m in range(1, line):
        w_line(m).start()

    def w_rep(m):
        return remote(
            wr_in.at[r], wr_in.at[r], ws.at[2, m], wr.at[2, r], partner(r, m), b
        )

    def w_sum_line():
        part = wl_out[0].astype(F32)
        for m in range(1, line):
            w_line(m).wait_recv()
            part = part + wl_in[m].astype(F32)
        wr_in[r] = part.astype(kind)
        for m in range(1, n_rep):
            w_rep(m).start()

    def w_back(m):
        return remote(
            wgath.at[c, z], wgath.at[c, z], ws.at[3, m], wr.at[3, z], r, blk_at(m)
        )

    def w_pass(m):
        place = partner(z, m)
        return remote(
            wgath.at[c, place], wgath.at[c, place], ws.at[4, m], wr.at[4, place], r, other
        )

    def w_sum_rep():
        for m in range(1, n_rep):
            peer = partner(r, m)
            arrive(wr_in.at[peer], ws.at[2, m], wr.at[2, peer], peer, b)
        part = wr_in[0].astype(F32)
        for i in range(1, n_rep):
            part = part + wr_in[i].astype(F32)
        wgath[c, z] = part.astype(kind)
        for m in range(1, line):
            w_back(m).start()
        w_pass(0).start()

    def b_sib(h, m):
        place = partner(z, m)
        return remote(
            bsib_out.at[place, :, cols(h)], bsib_in.at[place, :, cols(h)],
            bs.at[h, 0, m], br_sib.at[h, place], r, other,
        )

    def b_line(h, m):
        return remote(
            bout.at[m, :, cols(h)], bin_.at[m, :, cols(h)],
            bs.at[h, 1, m], br_line.at[h, m], r, blk_at(m),
        )

    def b_relay(h):
        return remote(
            bout.at[3, :, cols(h)], brelay.at[:, cols(h)],
            bs.at[h, 1, 3], br_relay.at[h], r, blk_at(2),
        )

    for h in range(pieces):
        if h:
            add_panel(h, r * group, group, gg[r, :, cols(h)], True)
        for m in range(1, n_rep):
            peer = partner(r, m)
            arrive(gg.at[peer, :, cols(h)], gs.at[h, m], gr.at[h, peer], peer, b)
            if m < n_rep - 1:
                add_panel(h, peer * group, group, gg[peer, :, cols(h)], False)
            if m == 1 and h == 0:
                w_sum_line()
        peer = partner(r, n_rep - 1)
        rhs = gg[peer, :, cols(h)]

        def finish(blk):
            at = pl.multiple_of(blk * rows, rows)
            panel = dense[pl.ds(pl.multiple_of(peer * group + blk * rows, rows), rows), :]
            return acc[pl.ds(at, rows), cols(h)] + jnp.dot(
                panel, rhs, preferred_element_type=F32
            )

        for m in range(line - 1, -1, -1):
            place = partner(z, m)
            bsib_out[place, :, cols(h)] = finish(place * 2 + 1 - c).astype(BF16)
            b_sib(h, m).start()
        if h == pieces - 1:
            w_sum_rep()
        for m in range(line - 1, -1, -1):
            place = partner(z, m)
            mine = finish(place * 2 + c)
            arrive(
                bsib_in.at[place, :, cols(h)], bs.at[h, 0, m], br_sib.at[h, place], r, other
            )
            mine = mine + bsib_in[place, :, cols(h)].astype(F32)
            if m == 0:
                fin[0, :, cols(h)] = mine
            elif relay and m == 3:
                bout[m, :, cols(h)] = mine.astype(BF16)

                @pl.when(outer)
                def _():
                    b_relay(h).start()

                @pl.when(jnp.logical_not(outer))
                def _():
                    b_line(h, m).start()
            elif relay and m == 1:
                fin[1, :, cols(h)] = mine

                @pl.when(jnp.logical_not(outer))
                def _():
                    b_relay(h).wait_recv()
                    fin[1, :, cols(h)] += brelay[:, cols(h)].astype(F32)

                bout[m, :, cols(h)] = fin[1, :, cols(h)].astype(BF16)
                b_line(h, m).start()
            else:
                bout[m, :, cols(h)] = mine.astype(BF16)
                b_line(h, m).start()

    for m in range(1, line):
        place = partner(z, m)
        arrive(wgath.at[c, place], ws.at[3, m], wr.at[3, place], r, blk_at(m))
        w_pass(m).start()
    for m in range(line):
        place = partner(z, m)
        arrive(wgath.at[1 - c, place], ws.at[4, m], wr.at[4, place], r, other)
    for core in range(2):
        for place in range(line):
            at = core * half + place * share
            gw_ref[at:at + share, :] = wgath[core, place].astype(F32)
    gw_out = pltpu.make_async_copy(gw_ref, gw_hbm, loc.at[6])
    gw_out.start()

    for h in range(pieces):
        for m in range(1, line):
            if relay and m == 3:
                @pl.when(jnp.logical_not(outer))
                def _():
                    b_line(h, m).wait_recv()
                    fin[0, :, cols(h)] += bin_[m, :, cols(h)].astype(F32)
            else:
                b_line(h, m).wait_recv()
                fin[0, :, cols(h)] += bin_[m, :, cols(h)].astype(F32)
    gf_ref[...] = fin[0].astype(BF16)
    gf_out = pltpu.make_async_copy(gf_ref, gf_hbm, loc.at[7])
    gf_out.start()

    for h in range(pieces):
        for m in range(1, line):
            if relay and m == 3:
                @pl.when(jnp.logical_not(outer))
                def _():
                    x_line(h, m).wait_send()
                    x_relay(h).wait_send()
            else:
                x_line(h, m).wait_send()
            b_line(h, m).wait_send()
        for m in range(line):
            x_pass(h, m).wait_send()
            b_sib(h, m).wait_send()
        for m in range(1, n_rep):
            p_send(h, m).wait_send()
            g_send(h, m).wait_send()
    w_sib.wait_send()
    for m in range(1, line):
        w_line(m).wait_send()
        w_back(m).wait_send()
    for m in range(line):
        w_pass(m).wait_send()
    for m in range(1, n_rep):
        w_rep(m).wait_send()


    for copy in (layer_out, gw_out, gf_out):
        copy.wait()


def hand_over(layer, gw, gf, layer_to, gw_to, gf_to, sems):
    copies = [
        pltpu.make_async_copy(src, dst, sems.at[i])
        for i, (src, dst) in enumerate([(layer, layer_to), (gw, gw_to), (gf, gf_to)])
    ]
    for copy in copies:
        copy.start()
    for copy in copies:
        copy.wait()


def on_device(n_rep, n_blk, node_features, tile_values, tile_row, tile_col, tile_count, weight, cotangent):
    rows, feats = node_features.shape
    slots, tile = tile_values.shape[2], tile_values.shape[3]
    slab_blocks = n_rep * rows // tile
    group_blocks = n_blk * rows // tile
    line = n_blk // 2
    share = feats // 2 // line
    kind = BF16 if share % 16 == 0 else F32
    pairs = slab_blocks * group_blocks
    table = (-(-pairs // 1024) * 8, 128)
    block = (rows, feats)
    h = PIECES
    dma = pltpu.SemaphoreType.DMA
    results = (
        jax.ShapeDtypeStruct(block, BF16),
        jax.ShapeDtypeStruct((feats, feats), F32),
        jax.ShapeDtypeStruct(block, BF16),
    )
    anywhere = pl.BlockSpec(memory_space=pl.ANY)
    scalars = pl.BlockSpec(memory_space=pltpu.SMEM)
    made = pl.pallas_call(
        functools.partial(kernel, n_rep, n_blk, h),
        out_shape=results,
        in_specs=[scalars] * 3 + [anywhere] * 4,
        out_specs=(anywhere,) * 3,
        scratch_shapes=[
            pltpu.VMEM(table, jnp.int32),
            pltpu.SMEM(table, jnp.int32),
            pltpu.VMEM(block, BF16),
            pltpu.VMEM((feats, feats), F32),
            pltpu.VMEM(block, BF16),
            pltpu.VMEM((slots + 1, tile, tile), BF16),
            pltpu.VMEM((n_blk * n_rep * rows, rows), BF16),
            pltpu.VMEM((n_blk,) + block, BF16),
            pltpu.VMEM((feats, feats), BF16),
            pltpu.VMEM(block, BF16),
            pltpu.VMEM((max(n_blk, n_rep) * rows, feats), F32),
            pltpu.VMEM((n_rep,) + block, BF16),
            pltpu.VMEM((n_rep,) + block, BF16),
            pltpu.VMEM((n_rep,) + block, BF16),
            pltpu.VMEM((line,) + block, BF16),
            pltpu.VMEM((line,) + block, BF16),
            pltpu.VMEM((line,) + block, BF16),
            pltpu.VMEM((line,) + block, BF16),
            pltpu.VMEM(block, BF16),
            pltpu.VMEM((feats // 2, feats), kind),
            pltpu.VMEM((feats // 2, feats), kind),
            pltpu.VMEM((line, share, feats), kind),
            pltpu.VMEM((line, share, feats), kind),
            pltpu.VMEM((n_rep, share, feats), kind),
            pltpu.VMEM((2, line, share, feats), kind),
            pltpu.VMEM((feats, feats), F32),
            pltpu.VMEM((2,) + block, F32),
            dma((8,)),
            dma((h, 2, line)),
            dma((h, n_blk)),
            dma((h, n_rep)),
            dma((h, n_rep)),
            dma((h, n_rep)),
            dma((h, n_rep)),
            dma((h, 2, line)),
            dma((h, line)),
            dma((h, line)),
            dma((h,)),
            dma((5, max(line, n_rep))),
            dma((5, max(line, n_rep))),
        ],
        compiler_params=pltpu.CompilerParams(
            collective_id=0, has_side_effects=True, vmem_limit_bytes=62 * 1024 * 1024
        ),
    )(
        tile_row[0, 0], tile_col[0, 0], tile_count, tile_values[0, 0],
        node_features, weight, cotangent[0, 0],
    )
    layer, gw, gf = pl.pallas_call(
        hand_over,
        out_shape=results,
        in_specs=[anywhere] * 3,
        out_specs=(anywhere,) * 3,
        scratch_shapes=[dma((3,))],
        compiler_params=pltpu.CompilerParams(vmem_limit_bytes=62 * 1024 * 1024),
    )(*made)
    return layer.reshape((1, 1) + block), gw, gf


def solution(mesh):
    placed = (
        P(("rep", "blk"), None),
        P("rep", "blk", None, None, None),
        P("rep", "blk", None),
        P("rep", "blk", None),
        P("rep", "blk"),
        P(),
        P("blk", "rep", None, None),
    )
    return jax.shard_map(
        functools.partial(on_device, mesh.shape["rep"], mesh.shape["blk"]),
        mesh=mesh,
        in_specs=placed,
        out_specs=(P("blk", "rep", None, None), P(), P(("rep", "blk"), None)),
        check_vma=False,
    )
```

```python
import functools

import jax
import jax.numpy as jnp
from jax import lax
from jax.experimental import pallas as pl
from jax.experimental.pallas import tpu as pltpu
from jax.sharding import PartitionSpec as P

MESH = pl.DeviceIdType.MESH
BF16, F32 = jnp.bfloat16, jnp.float32
PIECES = 2


def partner(index, step):
    out, bit = index, 1
    while bit <= step:
        if step & bit:
            out = out + bit * (1 - 2 * ((index // bit) % 2))
        bit *= 2
    return out


def kernel(
    n_rep, n_blk, pieces,
    row_ref, col_ref, count_ref, tiles_hbm, x_hbm, w_hbm, cot_hbm,
    layer_hbm, gw_hbm, gf_hbm,
    slot_vec, slot_ref, layer_ref, gw_ref, gf_ref,
    tiles, slabs, xg, w, cot, acc, pout, pin, gg, bsib_out, bsib_in, bout, bin_, brelay,
    wsib_out, wsib_in, wl_out, wl_in, wr_in, wgath, wpart, fin,
    loc, xs, xr, ps, pr, gs, gr, bs, br_sib, br_line, br_relay, ws, wr,
):
    rows, feats = x_hbm.shape
    tile = tiles.shape[1]
    dense, turned = slabs.at[0], slabs.at[slabs.shape[0] - 1]
    per = rows // tile
    line = n_blk // 2
    slab, group = rows * n_rep, rows * n_blk
    slab_blocks, group_blocks = slab // tile, group // tile
    fh = feats // pieces
    relay = line == 4
    r, b = lax.axis_index("rep"), lax.axis_index("blk")
    z, c = b // 2, b % 2
    other = b + 1 - 2 * c
    outer = jnp.logical_or(z == 0, z == line - 1)

    def blk_at(m):
        return partner(z, m) * 2 + c

    def remote(src, dst, send, recv, rep, blk):
        return pltpu.make_async_remote_copy(
            src_ref=src, dst_ref=dst, send_sem=send, recv_sem=recv,
            device_id={"rep": rep, "blk": blk}, device_id_type=MESH,
        )

    def arrive(dst, send, recv, rep, blk):
        remote(dst, dst, send, recv, rep, blk).wait_recv()

    fetch = [
        pltpu.make_async_copy(tiles_hbm, tiles.at[pl.ds(1, tiles.shape[0] - 1)], loc.at[1]),
        pltpu.make_async_copy(w_hbm, w, loc.at[2]),
        pltpu.make_async_copy(cot_hbm, cot, loc.at[3]),
    ]
    x_in = [
        pltpu.make_async_copy(x_hbm.at[:, pl.ds(h * fh, fh)], xg.at[b, h], loc.at[8 + h])
        for h in range(pieces)
    ]
    for copy in x_in + fetch:
        copy.start()

    barrier = pltpu.get_barrier_semaphore()
    friends = [(r, blk_at(m)) for m in range(1, line)] + [(r, other)]
    friends += [(partner(r, m), b) for m in range(1, n_rep)]
    for rep, blk in friends:
        pl.semaphore_signal(
            barrier, inc=1, device_id={"rep": rep, "blk": blk}, device_id_type=MESH
        )
    tiles[0] = jnp.zeros((tile, tile), BF16)

    shape = slot_vec.shape
    spots = lax.broadcasted_iota(jnp.int32, shape, 0) * shape[1] + lax.broadcasted_iota(
        jnp.int32, shape, 1
    )

    def mark(t, found):
        named = jnp.where(t < count_ref[0, 0], row_ref[t] * group_blocks + col_ref[t], -1)
        return jnp.where(spots == named, t + 1, found)

    slot_vec[...] = lax.fori_loop(
        0, row_ref.shape[0], mark, jnp.zeros(shape, jnp.int32), unroll=8
    )
    slots_in = pltpu.make_async_copy(slot_vec, slot_ref, loc.at[4])
    slots_in.start()
    pl.semaphore_wait(barrier, len(friends))

    def cols(h):
        return pl.ds(h * fh, fh)

    sends = []

    def x_line(h, m):
        return remote(
            xg.at[b, h], xg.at[b, h], xs.at[h, 0, m], xr.at[h, b], r, blk_at(m)
        )

    def x_relay(h):
        via = blk_at(2)
        return remote(
            xg.at[via, h], xg.at[via, h], xs.at[h, 0, 0], xr.at[h, via],
            r, blk_at(1),
        )

    def x_pass(h, m):
        blk = blk_at(m)
        src = xg.at[blk, h]
        return remote(
            src, xg.at[blk, h], xs.at[h, 1, m], xr.at[h, blk], r, other
        )

    for h in range(pieces):
        x_in[h].wait()
        for m in range(line - 1, 0, -1):
            if relay and m == 3:
                @pl.when(jnp.logical_not(outer))
                def _():
                    x_line(h, m).start()
            else:
                x_line(h, m).start()
        x_pass(h, 0).start()

    fetch[0].wait()
    slots_in.wait()

    def slot_at(pair):
        return slot_ref[pair // shape[1], pair % shape[1]]

    def lay_out(n, carry):
        panel, k = n // slab_blocks, n % slab_blocks
        for j in range(per):
            slot = slot_at(k * group_blocks + panel * per + j)
            start = pl.multiple_of(panel * slab + k * tile, tile)
            dense[pl.ds(start, tile), j * tile:(j + 1) * tile] = tiles[slot]
        return carry

    lax.fori_loop(0, n_blk * slab_blocks, lay_out, 0, unroll=4)

    def turn(t, carry):
        tiles[t] = tiles[t].T
        return carry

    def lay_out_turned(n, carry):
        panel, k = n // group_blocks, n % group_blocks
        for j in range(per):
            slot = slot_at((panel * per + j) * group_blocks + k)
            start = pl.multiple_of(panel * group + k * tile, tile)
            turned[pl.ds(start, tile), j * tile:(j + 1) * tile] = tiles[slot]
        return carry

    def steps(body, first, last, count, unroll):
        size = (last - first) // count
        return [
            functools.partial(
                lax.fori_loop, first + i * size, first + (i + 1) * size, body, 0, unroll=unroll
            )
            for i in range(count)
        ]

    later = steps(turn, 1, tiles.shape[0], 2, 2)
    later += steps(lay_out_turned, 0, n_rep * group_blocks, 4, 4)
    early = slabs.shape[0] > 1

    chunk = 4 * rows if slab % (4 * rows) == 0 else rows

    def add_panel(slabs, h, base, height, rhs, first):
        for at in range(0, height, chunk):
            lhs = slabs[pl.ds(pl.multiple_of(base + at, tile), chunk), :]
            part = jnp.dot(lhs, rhs, preferred_element_type=F32)
            if first:
                acc[pl.ds(at, chunk), cols(h)] = part
            else:
                acc[pl.ds(at, chunk), cols(h)] += part

    def p_send(h, m):
        to = partner(r, m)
        return remote(
            pout.at[to, h], pin.at[r, h], ps.at[h, m], pr.at[h, r], to, b
        )

    for h in range(pieces):
        add_panel(dense, h, b * slab, slab, xg[b, h], True)
        arrive(xg.at[other, h], xs.at[h, 1, 0], xr.at[h, other], r, other)
        add_panel(dense, h, other * slab, slab, xg[other, h], False)
        for m in range(1, line):
            blk = blk_at(m)
            arrive(xg.at[blk, h], xs.at[h, 0, m], xr.at[h, blk], r, blk)
            if relay and m == 2:
                @pl.when(jnp.logical_not(outer))
                def _():
                    x_relay(h).start()
            x_pass(h, m).start()
            add_panel(dense, h, blk * slab, slab, xg[blk, h], False)
            if early and later:
                later.pop(0)()
            if m > 1:
                last = partner(z, m - 1) * 2 + 1 - c
                arrive(xg.at[last, h], xs.at[h, 1, m - 1], xr.at[h, last], r, other)
                add_panel(dense, h, last * slab, slab, xg[last, h], False)
        last = partner(z, line - 1) * 2 + 1 - c
        arrive(xg.at[last, h], xs.at[h, 1, line - 1], xr.at[h, last], r, other)
        for m in range(n_rep - 1, -1, -1):
            to = partner(r, m)
            at = pl.multiple_of(to * rows, rows)
            panel = dense[pl.ds(pl.multiple_of(last * slab + to * rows, rows), rows), :]
            part = acc[pl.ds(at, rows), cols(h)] + jnp.dot(
                panel, xg[last, h], preferred_element_type=F32
            )
            pout[to, h] = part.astype(BF16)
            if m:
                p_send(h, m).start()

    while later:
        later.pop(0)()
    fetch[1].wait()
    fetch[2].wait()

    hidden, preact = [], 0.0
    for h in range(pieces):
        total = pout[r, h].astype(F32)
        for m in range(1, n_rep):
            peer = partner(r, m)
            arrive(pin.at[peer, h], ps.at[h, m], pr.at[h, peer], peer, b)
            total = total + pin[peer, h].astype(F32)
        hidden.append(total.astype(BF16))
        preact += jnp.dot(hidden[h], w[cols(h), :], preferred_element_type=F32)
    gate = jax.nn.sigmoid(preact)
    slope = gate * (1.0 + preact * (1.0 - gate))
    grad_pre = (cot[...].astype(F32) * slope).astype(BF16)

    def g_send(h, m):
        to = partner(r, m)
        return remote(
            gg.at[r, h], gg.at[r, h], gs.at[h, m], gr.at[h, r], to, b
        )

    for h in range(pieces):
        gg[r, h] = lax.dot_general(
            grad_pre, w[cols(h), :], (((1,), (1,)), ((), ())), preferred_element_type=F32
        ).astype(BF16)
        for m in range(n_rep - 1, 0, -1):
            g_send(h, m).start()

    layer_ref[...] = (preact * gate).astype(BF16)
    layer_out = pltpu.make_async_copy(layer_ref, layer_hbm, loc.at[5])
    layer_out.start()
    for h in range(pieces):
        wpart[cols(h), :] = lax.dot_general(
            hidden[h], grad_pre, (((0,), (0,)), ((), ())), preferred_element_type=F32
        )
    half = feats // 2
    share = half // line
    kind = wl_out.dtype
    mine_at, other_at = c * half, (1 - c) * half
    wsib_out[...] = wpart[pl.ds(pl.multiple_of(other_at, half), half), :].astype(kind)
    w_sib = remote(wsib_out, wsib_in, ws.at[0, 0], wr.at[0, 0], r, other)
    w_sib.start()

    add_panel(turned, 0, r * group, group, gg[r, 0], True)

    w_sib.wait_recv()
    both = wpart[pl.ds(pl.multiple_of(mine_at, half), half), :] + wsib_in[...].astype(F32)
    wpart[pl.ds(0, half), :] = both
    for m in range(line):
        at = pl.multiple_of(partner(z, m) * share, share)
        wl_out[m] = wpart[pl.ds(at, share), :].astype(kind)

    def w_line(m):
        return remote(wl_out.at[m], wl_in.at[m], ws.at[1, m], wr.at[1, m], r, blk_at(m))

    for m in range(1, line):
        w_line(m).start()

    def w_rep(m):
        return remote(
            wr_in.at[r], wr_in.at[r], ws.at[2, m], wr.at[2, r], partner(r, m), b
        )

    def w_sum_line():
        part = wl_out[0].astype(F32)
        for m in range(1, line):
            w_line(m).wait_recv()
            part = part + wl_in[m].astype(F32)
        wr_in[r] = part.astype(kind)
        for m in range(1, n_rep):
            w_rep(m).start()

    def w_back(m):
        return remote(
            wgath.at[c, z], wgath.at[c, z], ws.at[3, m], wr.at[3, z], r, blk_at(m)
        )

    def w_pass(m):
        place = partner(z, m)
        return remote(
            wgath.at[c, place], wgath.at[c, place], ws.at[4, m], wr.at[4, place], r, other
        )

    def w_sum_rep():
        for m in range(1, n_rep):
            peer = partner(r, m)
            arrive(wr_in.at[peer], ws.at[2, m], wr.at[2, peer], peer, b)
        part = wr_in[0].astype(F32)
        for i in range(1, n_rep):
            part = part + wr_in[i].astype(F32)
        wgath[c, z] = part.astype(kind)
        for m in range(1, line):
            w_back(m).start()
        w_pass(0).start()

    def b_sib(h, m):
        place = partner(z, m)
        return remote(
            bsib_out.at[place, h], bsib_in.at[place, h],
            bs.at[h, 0, m], br_sib.at[h, place], r, other,
        )

    def b_line(h, m):
        return remote(
            bout.at[m, h], bin_.at[m, h],
            bs.at[h, 1, m], br_line.at[h, m], r, blk_at(m),
        )

    def b_relay(h):
        return remote(
            bout.at[3, h], brelay.at[h],
            bs.at[h, 1, 3], br_relay.at[h], r, blk_at(2),
        )

    tail = n_rep - 1

    def finish(h, blk):
        peer = partner(r, tail)
        at = pl.multiple_of(blk * rows, rows)
        panel = turned[pl.ds(pl.multiple_of(peer * group + blk * rows, rows), rows), :]
        return acc[pl.ds(at, rows), cols(h)] + jnp.dot(
            panel, gg[peer, h], preferred_element_type=F32
        )

    def back_terms(h):
        if h:
            add_panel(turned, h, r * group, group, gg[r, h], True)
        for m in range(1, n_rep):
            peer = partner(r, m)
            arrive(gg.at[peer, h], gs.at[h, m], gr.at[h, peer], peer, b)
            if m < tail:
                add_panel(turned, h, peer * group, group, gg[peer, h], False)
        for m in range(line - 1, -1, -1):
            place = partner(z, m)
            bsib_out[place, h] = finish(h, place * 2 + 1 - c).astype(BF16)
            b_sib(h, m).start()

    def chip_sum(h, m):
        place = partner(z, m)
        mine = finish(h, place * 2 + c)
        arrive(bsib_in.at[place, h], bs.at[h, 0, m], br_sib.at[h, place], r, other)
        return mine + bsib_in[place, h].astype(F32)

    def send_far(h):
        for m in range(line - 1, 1, -1):
            bout[m, h] = chip_sum(h, m).astype(BF16)
            if relay and m == 3:
                @pl.when(outer)
                def _():
                    b_relay(h).start()

                @pl.when(jnp.logical_not(outer))
                def _():
                    b_line(h, m).start()
            else:
                b_line(h, m).start()
        fin[1, :, cols(h)] = chip_sum(h, 1)
        fin[0, :, cols(h)] = chip_sum(h, 0)

    def send_near(h):
        if relay:
            @pl.when(jnp.logical_not(outer))
            def _():
                b_relay(h).wait_recv()
                fin[1, :, cols(h)] += brelay[h].astype(F32)

        bout[1, h] = fin[1, :, cols(h)].astype(BF16)
        b_line(h, 1).start()

    for h in range(pieces):
        back_terms(h)
        if h == 0:
            w_sum_line()
        else:
            send_near(h - 1)
        if h == pieces - 1:
            w_sum_rep()
        send_far(h)
    send_near(pieces - 1)

    for m in range(1, line):
        place = partner(z, m)
        arrive(wgath.at[c, place], ws.at[3, m], wr.at[3, place], r, blk_at(m))
        w_pass(m).start()
    for m in range(line):
        place = partner(z, m)
        arrive(wgath.at[1 - c, place], ws.at[4, m], wr.at[4, place], r, other)
    for core in range(2):
        for place in range(line):
            at = core * half + place * share
            gw_ref[at:at + share, :] = wgath[core, place].astype(F32)
    gw_out = pltpu.make_async_copy(gw_ref, gw_hbm, loc.at[6])
    gw_out.start()

    for h in range(pieces):
        for m in range(1, line):
            if relay and m == 3:
                @pl.when(jnp.logical_not(outer))
                def _():
                    b_line(h, m).wait_recv()
                    fin[0, :, cols(h)] += bin_[m, h].astype(F32)
            else:
                b_line(h, m).wait_recv()
                fin[0, :, cols(h)] += bin_[m, h].astype(F32)
    gf_ref[...] = fin[0].astype(BF16)
    gf_out = pltpu.make_async_copy(gf_ref, gf_hbm, loc.at[7])
    gf_out.start()

    for h in range(pieces):
        for m in range(1, line):
            if relay and m == 3:
                @pl.when(jnp.logical_not(outer))
                def _():
                    x_line(h, m).wait_send()
                    x_relay(h).wait_send()
            else:
                x_line(h, m).wait_send()
            b_line(h, m).wait_send()
        for m in range(line):
            x_pass(h, m).wait_send()
            b_sib(h, m).wait_send()
        for m in range(1, n_rep):
            p_send(h, m).wait_send()
            g_send(h, m).wait_send()
    w_sib.wait_send()
    for m in range(1, line):
        w_line(m).wait_send()
        w_back(m).wait_send()
    for m in range(line):
        w_pass(m).wait_send()
    for m in range(1, n_rep):
        w_rep(m).wait_send()


    for copy in (layer_out, gw_out, gf_out):
        copy.wait()


def hand_over(layer, gw, gf, layer_to, gw_to, gf_to, layer_at, gw_at, gf_at, sems):
    trips = [(layer, layer_at, layer_to), (gw, gw_at, gw_to), (gf, gf_at, gf_to)]
    inward = [pltpu.make_async_copy(a, b, sems.at[0, i]) for i, (a, b, _) in enumerate(trips)]
    outward = [pltpu.make_async_copy(b, c, sems.at[1, i]) for i, (_, b, c) in enumerate(trips)]
    for copy in inward:
        copy.start()
    for first, second in zip(inward, outward):
        first.wait()
        second.start()
    for copy in outward:
        copy.wait()


def on_device(n_rep, n_blk, node_features, tile_values, tile_row, tile_col, tile_count, weight, cotangent):
    rows, feats = node_features.shape
    slots, tile = tile_values.shape[2], tile_values.shape[3]
    slab_blocks = n_rep * rows // tile
    group_blocks = n_blk * rows // tile
    line = n_blk // 2
    share = feats // 2 // line
    kind = BF16 if share % 16 == 0 else F32
    pairs = slab_blocks * group_blocks
    table = (-(-pairs // 1024) * 8, 128)
    block = (rows, feats)
    h = PIECES
    piece = (h, rows, feats // h)
    slab_size = n_blk * n_rep * rows
    copies = 2 if slab_size * rows * 4 <= 24 * 1024 * 1024 else 1
    dma = pltpu.SemaphoreType.DMA
    results = (
        jax.ShapeDtypeStruct(block, BF16),
        jax.ShapeDtypeStruct((feats, feats), F32),
        jax.ShapeDtypeStruct(block, BF16),
    )
    anywhere = pl.BlockSpec(memory_space=pl.ANY)
    scalars = pl.BlockSpec(memory_space=pltpu.SMEM)
    made = pl.pallas_call(
        functools.partial(kernel, n_rep, n_blk, h),
        out_shape=results,
        in_specs=[scalars] * 3 + [anywhere] * 4,
        out_specs=(anywhere,) * 3,
        scratch_shapes=[
            pltpu.VMEM(table, jnp.int32),
            pltpu.SMEM(table, jnp.int32),
            pltpu.VMEM(block, BF16),
            pltpu.VMEM((feats, feats), F32),
            pltpu.VMEM(block, BF16),
            pltpu.VMEM((slots + 1, tile, tile), BF16),
            pltpu.VMEM((copies, slab_size, rows), BF16),
            pltpu.VMEM((n_blk,) + piece, BF16),
            pltpu.VMEM((feats, feats), BF16),
            pltpu.VMEM(block, BF16),
            pltpu.VMEM((max(n_blk, n_rep) * rows, feats), F32),
            pltpu.VMEM((n_rep,) + piece, BF16),
            pltpu.VMEM((n_rep,) + piece, BF16),
            pltpu.VMEM((n_rep,) + piece, BF16),
            pltpu.VMEM((line,) + piece, BF16),
            pltpu.VMEM((line,) + piece, BF16),
            pltpu.VMEM((line,) + piece, BF16),
            pltpu.VMEM((line,) + piece, BF16),
            pltpu.VMEM(piece, BF16),
            pltpu.VMEM((feats // 2, feats), kind),
            pltpu.VMEM((feats // 2, feats), kind),
            pltpu.VMEM((line, share, feats), kind),
            pltpu.VMEM((line, share, feats), kind),
            pltpu.VMEM((n_rep, share, feats), kind),
            pltpu.VMEM((2, line, share, feats), kind),
            pltpu.VMEM((feats, feats), F32),
            pltpu.VMEM((2,) + block, F32),
            dma((8 + h,)),
            dma((h, 2, line)),
            dma((h, n_blk)),
            dma((h, n_rep)),
            dma((h, n_rep)),
            dma((h, n_rep)),
            dma((h, n_rep)),
            dma((h, 2, line)),
            dma((h, line)),
            dma((h, line)),
            dma((h,)),
            dma((5, max(line, n_rep))),
            dma((5, max(line, n_rep))),
        ],
        compiler_params=pltpu.CompilerParams(
            collective_id=0, has_side_effects=True, vmem_limit_bytes=62 * 1024 * 1024
        ),
    )(
        tile_row[0, 0], tile_col[0, 0], tile_count, tile_values[0, 0],
        node_features, weight, cotangent[0, 0],
    )
    layer, gw, gf = pl.pallas_call(
        hand_over,
        out_shape=results,
        in_specs=[anywhere] * 3,
        out_specs=(anywhere,) * 3,
        scratch_shapes=[pltpu.VMEM(made[i].shape, made[i].dtype) for i in range(3)] + [dma((2, 3))],
        compiler_params=pltpu.CompilerParams(vmem_limit_bytes=62 * 1024 * 1024),
    )(*made)
    return layer.reshape((1, 1) + block), gw, gf


def solution(mesh):
    placed = (
        P(("rep", "blk"), None),
        P("rep", "blk", None, None, None),
        P("rep", "blk", None),
        P("rep", "blk", None),
        P("rep", "blk"),
        P(),
        P("blk", "rep", None, None),
    )
    return jax.shard_map(
        functools.partial(on_device, mesh.shape["rep"], mesh.shape["blk"]),
        mesh=mesh,
        in_specs=placed,
        out_specs=(P("blk", "rep", None, None), P(), P(("rep", "blk"), None)),
        check_vma=False,
    )
```

```python
import functools

import jax
import jax.numpy as jnp
from jax import lax
from jax.experimental import pallas as pl
from jax.experimental.pallas import tpu as pltpu
from jax.sharding import PartitionSpec as P

MESH = pl.DeviceIdType.MESH
BF16, F32 = jnp.bfloat16, jnp.float32
PIECES = 2
CHUNK = 256


def partner(index, step, bits=8):
    out = index
    for bit in [2**i for i in range(bits)]:
        flip = 1 - 2 * ((index // bit) % 2)
        if isinstance(step, int):
            out = out + bit * flip if step & bit else out
        else:
            out = out + bit * flip * ((step // bit) % 2)
    return out


def kernel(
    n_rep, n_blk, pieces,
    row_ref, col_ref, count_ref, tiles_hbm, x_hbm, w_hbm, cot_hbm,
    layer_hbm, gw_hbm, gf_hbm,
    slot_vec, slot_ref, layer_ref, gw_ref, gf_ref,
    tiles, slabs, xg, w, cot, acc, pout, pin, gg, bsib_out, bsib_in, bout, bin_, brelay,
    wsib_out, wsib_in, wl_out, wl_in, wr_in, wgath, wpart, fin,
    loc, xs, xr, ps, pr, gs, gr, bs, br_sib, br_line, br_relay, ws, wr,
):
    rows, feats = x_hbm.shape
    tile = tiles.shape[1]
    dense, turned = slabs.at[0], slabs.at[slabs.shape[0] - 1]
    per = rows // tile
    line = n_blk // 2
    slab, group = rows * n_rep, rows * n_blk
    slab_blocks, group_blocks = slab // tile, group // tile
    fh = feats // pieces
    relay = line == 4
    r, b = lax.axis_index("rep"), lax.axis_index("blk")
    z, c = b // 2, b % 2
    other = b + 1 - 2 * c
    outer = jnp.logical_or(z == 0, z == line - 1)

    def blk_at(m):
        return partner(z, m) * 2 + c

    def remote(src, dst, send, recv, rep, blk):
        return pltpu.make_async_remote_copy(
            src_ref=src, dst_ref=dst, send_sem=send, recv_sem=recv,
            device_id={"rep": rep, "blk": blk}, device_id_type=MESH,
        )

    def arrive(dst, send, recv, rep, blk):
        remote(dst, dst, send, recv, rep, blk).wait_recv()

    fetch = [
        pltpu.make_async_copy(tiles_hbm, tiles.at[pl.ds(1, tiles.shape[0] - 1)], loc.at[1]),
        pltpu.make_async_copy(w_hbm, w, loc.at[2]),
        pltpu.make_async_copy(cot_hbm, cot, loc.at[3]),
    ]
    x_in = [
        pltpu.make_async_copy(x_hbm.at[:, pl.ds(h * fh, fh)], xg.at[b, h], loc.at[8 + h])
        for h in range(pieces)
    ]
    for copy in x_in + fetch:
        copy.start()

    barrier = pltpu.get_barrier_semaphore()
    friends = [(r, blk_at(m)) for m in range(1, line)] + [(r, other)]
    friends += [(partner(r, m), b) for m in range(1, n_rep)]
    for rep, blk in friends:
        pl.semaphore_signal(
            barrier, inc=1, device_id={"rep": rep, "blk": blk}, device_id_type=MESH
        )
    tiles[0] = jnp.zeros((tile, tile), BF16)

    shape = slot_vec.shape
    spots = lax.broadcasted_iota(jnp.int32, shape, 0) * shape[1] + lax.broadcasted_iota(
        jnp.int32, shape, 1
    )

    def mark(t, found):
        named = jnp.where(t < count_ref[0, 0], row_ref[t] * group_blocks + col_ref[t], -1)
        return jnp.where(spots == named, t + 1, found)

    slot_vec[...] = lax.fori_loop(
        0, row_ref.shape[0], mark, jnp.zeros(shape, jnp.int32), unroll=8
    )
    slots_in = pltpu.make_async_copy(slot_vec, slot_ref, loc.at[4])
    slots_in.start()
    pl.semaphore_wait(barrier, len(friends))

    def cols(h):
        return pl.ds(h * fh, fh)

    sends = []

    def x_line(h, m):
        return remote(
            xg.at[b, h], xg.at[b, h], xs.at[h, 0, m], xr.at[h, b], r, blk_at(m)
        )

    def x_relay(h):
        via = blk_at(2)
        return remote(
            xg.at[via, h], xg.at[via, h], xs.at[h, 0, 0], xr.at[h, via],
            r, blk_at(1),
        )

    def x_pass(h, m):
        blk = blk_at(m)
        src = xg.at[blk, h]
        return remote(
            src, xg.at[blk, h], xs.at[h, 1, m], xr.at[h, blk], r, other
        )

    for h in range(pieces):
        x_in[h].wait()
        for m in range(line - 1, 0, -1):
            if relay and m == 3:
                @pl.when(jnp.logical_not(outer))
                def _():
                    x_line(h, m).start()
            else:
                x_line(h, m).start()
        x_pass(h, 0).start()

    fetch[0].wait()
    slots_in.wait()

    def slot_at(pair):
        return slot_ref[pair // shape[1], pair % shape[1]]

    def lay_out(n, carry):
        panel, k = n // slab_blocks, n % slab_blocks
        for j in range(per):
            slot = slot_at(k * group_blocks + panel * per + j)
            start = pl.multiple_of(panel * slab + k * tile, tile)
            dense[pl.ds(start, tile), j * tile:(j + 1) * tile] = tiles[slot]
        return carry

    lax.fori_loop(0, n_blk * slab_blocks, lay_out, 0, unroll=2)

    def turn(t, carry):
        tiles[t] = tiles[t].T
        return carry

    def lay_out_turned(n, carry):
        panel, k = n // group_blocks, n % group_blocks
        for j in range(per):
            slot = slot_at((panel * per + j) * group_blocks + k)
            start = pl.multiple_of(panel * group + k * tile, tile)
            turned[pl.ds(start, tile), j * tile:(j + 1) * tile] = tiles[slot]
        return carry

    def steps(body, first, last, count, unroll):
        size = (last - first) // count
        return [
            functools.partial(
                lax.fori_loop, first + i * size, first + (i + 1) * size, body, 0, unroll=unroll
            )
            for i in range(count)
        ]

    later = steps(turn, 1, tiles.shape[0], 2, 1)
    later += steps(lay_out_turned, 0, n_rep * group_blocks, 4, 2)
    early = slabs.shape[0] > 1

    def add_panel(slab_ref, h, base, height, rhs_ref, first):
        def add(i, carry):
            at = pl.multiple_of(i * CHUNK, CHUNK)
            lhs = slab_ref[pl.ds(pl.multiple_of(base + i * CHUNK, tile), CHUNK), :]
            part = jnp.dot(lhs, rhs_ref[...], preferred_element_type=F32)
            if first:
                acc[pl.ds(at, CHUNK), cols(h)] = part
            else:
                acc[pl.ds(at, CHUNK), cols(h)] += part
            return carry

        lax.fori_loop(0, height // CHUNK, add, 0)

    def p_send(h, m):
        to = partner(r, m, 3)
        return remote(
            pout.at[to, h], pin.at[r, h], ps.at[h, m], pr.at[h, r], to, b
        )

    for h in range(pieces):
        add_panel(dense, h, b * slab, slab, xg.at[b, h], True)
        arrive(xg.at[other, h], xs.at[h, 1, 0], xr.at[h, other], r, other)
        add_panel(dense, h, other * slab, slab, xg.at[other, h], False)
        for m in range(1, line):
            blk = blk_at(m)
            arrive(xg.at[blk, h], xs.at[h, 0, m], xr.at[h, blk], r, blk)
            if relay and m == 2:
                @pl.when(jnp.logical_not(outer))
                def _():
                    x_relay(h).start()
            x_pass(h, m).start()
            add_panel(dense, h, blk * slab, slab, xg.at[blk, h], False)
            if early and later:
                later.pop(0)()
            if m > 1:
                last = partner(z, m - 1) * 2 + 1 - c
                arrive(xg.at[last, h], xs.at[h, 1, m - 1], xr.at[h, last], r, other)
                add_panel(dense, h, last * slab, slab, xg.at[last, h], False)
        last = partner(z, line - 1) * 2 + 1 - c
        arrive(xg.at[last, h], xs.at[h, 1, line - 1], xr.at[h, last], r, other)
        def last_panel(i, carry):
            m = n_rep - 1 - i
            to = partner(r, m, 3)
            at = pl.multiple_of(to * rows, rows)
            panel = dense[pl.ds(pl.multiple_of(last * slab + to * rows, rows), rows), :]
            part = acc[pl.ds(at, rows), cols(h)] + jnp.dot(
                panel, xg[last, h], preferred_element_type=F32
            )
            pout[to, h] = part.astype(BF16)

            @pl.when(m > 0)
            def _():
                p_send(h, m).start()

            return carry

        lax.fori_loop(0, n_rep, last_panel, 0)

    while later:
        later.pop(0)()
    fetch[1].wait()
    fetch[2].wait()

    hidden, preact = [], 0.0
    for h in range(pieces):
        total = pout[r, h].astype(F32)
        for m in range(1, n_rep):
            peer = partner(r, m)
            arrive(pin.at[peer, h], ps.at[h, m], pr.at[h, peer], peer, b)
            total = total + pin[peer, h].astype(F32)
        hidden.append(total.astype(BF16))
        preact += jnp.dot(hidden[h], w[cols(h), :], preferred_element_type=F32)
    gate = jax.nn.sigmoid(preact)
    slope = gate * (1.0 + preact * (1.0 - gate))
    grad_pre = (cot[...].astype(F32) * slope).astype(BF16)

    def g_send(h, m):
        to = partner(r, m)
        return remote(
            gg.at[r, h], gg.at[r, h], gs.at[h, m], gr.at[h, r], to, b
        )

    for h in range(pieces):
        gg[r, h] = lax.dot_general(
            grad_pre, w[cols(h), :], (((1,), (1,)), ((), ())), preferred_element_type=F32
        ).astype(BF16)
        for m in range(n_rep - 1, 0, -1):
            g_send(h, m).start()

    layer_ref[...] = (preact * gate).astype(BF16)
    layer_out = pltpu.make_async_copy(layer_ref, layer_hbm, loc.at[5])
    layer_out.start()
    for h in range(pieces):
        wpart[cols(h), :] = lax.dot_general(
            hidden[h], grad_pre, (((0,), (0,)), ((), ())), preferred_element_type=F32
        )
    half = feats // 2
    share = half // line
    kind = wl_out.dtype
    mine_at, other_at = c * half, (1 - c) * half
    wsib_out[...] = wpart[pl.ds(pl.multiple_of(other_at, half), half), :].astype(kind)
    w_sib = remote(wsib_out, wsib_in, ws.at[0, 0], wr.at[0, 0], r, other)
    w_sib.start()

    add_panel(turned, 0, r * group, group, gg.at[r, 0], True)

    w_sib.wait_recv()
    both = wpart[pl.ds(pl.multiple_of(mine_at, half), half), :] + wsib_in[...].astype(F32)
    wpart[pl.ds(0, half), :] = both
    for m in range(line):
        at = pl.multiple_of(partner(z, m) * share, share)
        wl_out[m] = wpart[pl.ds(at, share), :].astype(kind)

    def w_line(m):
        return remote(wl_out.at[m], wl_in.at[m], ws.at[1, m], wr.at[1, m], r, blk_at(m))

    for m in range(1, line):
        w_line(m).start()

    def w_rep(m):
        return remote(
            wr_in.at[r], wr_in.at[r], ws.at[2, m], wr.at[2, r], partner(r, m), b
        )

    def w_sum_line():
        part = wl_out[0].astype(F32)
        for m in range(1, line):
            w_line(m).wait_recv()
            part = part + wl_in[m].astype(F32)
        wr_in[r] = part.astype(kind)
        for m in range(1, n_rep):
            w_rep(m).start()

    def w_back(m):
        return remote(
            wgath.at[c, z], wgath.at[c, z], ws.at[3, m], wr.at[3, z], r, blk_at(m)
        )

    def w_pass(m):
        place = partner(z, m)
        return remote(
            wgath.at[c, place], wgath.at[c, place], ws.at[4, m], wr.at[4, place], r, other
        )

    def w_sum_rep():
        for m in range(1, n_rep):
            peer = partner(r, m)
            arrive(wr_in.at[peer], ws.at[2, m], wr.at[2, peer], peer, b)
        part = wr_in[0].astype(F32)
        for i in range(1, n_rep):
            part = part + wr_in[i].astype(F32)
        wgath[c, z] = part.astype(kind)
        for m in range(1, line):
            w_back(m).start()
        w_pass(0).start()

    def b_sib(h, m):
        place = partner(z, m, 4)
        return remote(
            bsib_out.at[place, h], bsib_in.at[place, h],
            bs.at[h, 0, m], br_sib.at[h, place], r, other,
        )

    def b_line(h, m):
        return remote(
            bout.at[m, h], bin_.at[m, h],
            bs.at[h, 1, m], br_line.at[h, m], r, blk_at(m),
        )

    def b_relay(h):
        return remote(
            bout.at[3, h], brelay.at[h],
            bs.at[h, 1, 3], br_relay.at[h], r, blk_at(2),
        )

    tail = n_rep - 1

    def finish(h, blk):
        peer = partner(r, tail)
        at = pl.multiple_of(blk * rows, rows)
        panel = turned[pl.ds(pl.multiple_of(peer * group + blk * rows, rows), rows), :]
        return acc[pl.ds(at, rows), cols(h)] + jnp.dot(
            panel, gg[peer, h], preferred_element_type=F32
        )

    def back_terms(h):
        if h:
            add_panel(turned, h, r * group, group, gg.at[r, h], True)
        for m in range(1, n_rep):
            peer = partner(r, m)
            arrive(gg.at[peer, h], gs.at[h, m], gr.at[h, peer], peer, b)
            if m < tail:
                add_panel(turned, h, peer * group, group, gg.at[peer, h], False)

        def to_sibling(i, carry):
            m = line - 1 - i
            place = partner(z, m, 4)
            bsib_out[place, h] = finish(h, place * 2 + 1 - c).astype(BF16)
            b_sib(h, m).start()
            return carry

        def keep(i, carry):
            blk = i * 2 + c
            acc[pl.ds(pl.multiple_of(blk * rows, rows), rows), cols(h)] = finish(h, blk)
            return carry

        lax.fori_loop(0, line, to_sibling, 0)
        lax.fori_loop(0, line, keep, 0)

    def chip_sum(h, m):
        place = partner(z, m)
        mine = acc[pl.ds(pl.multiple_of((place * 2 + c) * rows, rows), rows), cols(h)]
        arrive(bsib_in.at[place, h], bs.at[h, 0, m], br_sib.at[h, place], r, other)
        return mine + bsib_in[place, h].astype(F32)

    def send_far(h):
        for m in range(line - 1, 1, -1):
            bout[m, h] = chip_sum(h, m).astype(BF16)
            if relay and m == 3:
                @pl.when(outer)
                def _():
                    b_relay(h).start()

                @pl.when(jnp.logical_not(outer))
                def _():
                    b_line(h, m).start()
            else:
                b_line(h, m).start()
        fin[1, :, cols(h)] = chip_sum(h, 1)
        fin[0, :, cols(h)] = chip_sum(h, 0)

    def send_near(h):
        if relay:
            @pl.when(jnp.logical_not(outer))
            def _():
                b_relay(h).wait_recv()
                fin[1, :, cols(h)] += brelay[h].astype(F32)

        bout[1, h] = fin[1, :, cols(h)].astype(BF16)
        b_line(h, 1).start()

    for h in range(pieces):
        back_terms(h)
        if h == 0:
            w_sum_line()
        else:
            send_near(h - 1)
        if h == pieces - 1:
            w_sum_rep()
        send_far(h)
    send_near(pieces - 1)

    for m in range(1, line):
        place = partner(z, m)
        arrive(wgath.at[c, place], ws.at[3, m], wr.at[3, place], r, blk_at(m))
        w_pass(m).start()
    for m in range(line):
        place = partner(z, m)
        arrive(wgath.at[1 - c, place], ws.at[4, m], wr.at[4, place], r, other)
    for core in range(2):
        for place in range(line):
            at = core * half + place * share
            gw_ref[at:at + share, :] = wgath[core, place].astype(F32)
    gw_out = pltpu.make_async_copy(gw_ref, gw_hbm, loc.at[6])
    gw_out.start()

    for h in range(pieces):
        for m in range(1, line):
            if relay and m == 3:
                @pl.when(jnp.logical_not(outer))
                def _():
                    b_line(h, m).wait_recv()
                    fin[0, :, cols(h)] += bin_[m, h].astype(F32)
            else:
                b_line(h, m).wait_recv()
                fin[0, :, cols(h)] += bin_[m, h].astype(F32)
    gf_ref[...] = fin[0].astype(BF16)
    gf_out = pltpu.make_async_copy(gf_ref, gf_hbm, loc.at[7])
    gf_out.start()

    for h in range(pieces):
        for m in range(1, line):
            if relay and m == 3:
                @pl.when(jnp.logical_not(outer))
                def _():
                    x_line(h, m).wait_send()
                    x_relay(h).wait_send()
            else:
                x_line(h, m).wait_send()
            b_line(h, m).wait_send()
        for m in range(line):
            x_pass(h, m).wait_send()
            b_sib(h, m).wait_send()
        for m in range(1, n_rep):
            p_send(h, m).wait_send()
            g_send(h, m).wait_send()
    w_sib.wait_send()
    for m in range(1, line):
        w_line(m).wait_send()
        w_back(m).wait_send()
    for m in range(line):
        w_pass(m).wait_send()
    for m in range(1, n_rep):
        w_rep(m).wait_send()


    for copy in (layer_out, gw_out, gf_out):
        copy.wait()


def hand_over(layer, gw, gf, layer_to, gw_to, gf_to, layer_at, gw_at, gf_at, sems):
    trips = [(layer, layer_at, layer_to), (gw, gw_at, gw_to), (gf, gf_at, gf_to)]
    inward = [pltpu.make_async_copy(a, b, sems.at[0, i]) for i, (a, b, _) in enumerate(trips)]
    outward = [pltpu.make_async_copy(b, c, sems.at[1, i]) for i, (_, b, c) in enumerate(trips)]
    for copy in inward:
        copy.start()
    for first, second in zip(inward, outward):
        first.wait()
        second.start()
    for copy in outward:
        copy.wait()


def on_device(n_rep, n_blk, node_features, tile_values, tile_row, tile_col, tile_count, weight, cotangent):
    rows, feats = node_features.shape
    slots, tile = tile_values.shape[2], tile_values.shape[3]
    slab_blocks = n_rep * rows // tile
    group_blocks = n_blk * rows // tile
    line = n_blk // 2
    share = feats // 2 // line
    kind = BF16 if share % 16 == 0 else F32
    pairs = slab_blocks * group_blocks
    table = (-(-pairs // 1024) * 8, 128)
    block = (rows, feats)
    h = PIECES
    piece = (h, rows, feats // h)
    slab_size = n_blk * n_rep * rows
    copies = 2 if slab_size * rows * 4 <= 24 * 1024 * 1024 else 1
    dma = pltpu.SemaphoreType.DMA
    results = (
        jax.ShapeDtypeStruct(block, BF16),
        jax.ShapeDtypeStruct((feats, feats), F32),
        jax.ShapeDtypeStruct(block, BF16),
    )
    anywhere = pl.BlockSpec(memory_space=pl.ANY)
    scalars = pl.BlockSpec(memory_space=pltpu.SMEM)
    made = pl.pallas_call(
        functools.partial(kernel, n_rep, n_blk, h),
        out_shape=results,
        in_specs=[scalars] * 3 + [anywhere] * 4,
        out_specs=(anywhere,) * 3,
        scratch_shapes=[
            pltpu.VMEM(table, jnp.int32),
            pltpu.SMEM(table, jnp.int32),
            pltpu.VMEM(block, BF16),
            pltpu.VMEM((feats, feats), F32),
            pltpu.VMEM(block, BF16),
            pltpu.VMEM((slots + 1, tile, tile), BF16),
            pltpu.VMEM((copies, slab_size, rows), BF16),
            pltpu.VMEM((n_blk,) + piece, BF16),
            pltpu.VMEM((feats, feats), BF16),
            pltpu.VMEM(block, BF16),
            pltpu.VMEM((max(n_blk, n_rep) * rows, feats), F32),
            pltpu.VMEM((n_rep,) + piece, BF16),
            pltpu.VMEM((n_rep,) + piece, BF16),
            pltpu.VMEM((n_rep,) + piece, BF16),
            pltpu.VMEM((line,) + piece, BF16),
            pltpu.VMEM((line,) + piece, BF16),
            pltpu.VMEM((line,) + piece, BF16),
            pltpu.VMEM((line,) + piece, BF16),
            pltpu.VMEM(piece, BF16),
            pltpu.VMEM((feats // 2, feats), kind),
            pltpu.VMEM((feats // 2, feats), kind),
            pltpu.VMEM((line, share, feats), kind),
            pltpu.VMEM((line, share, feats), kind),
            pltpu.VMEM((n_rep, share, feats), kind),
            pltpu.VMEM((2, line, share, feats), kind),
            pltpu.VMEM((feats, feats), F32),
            pltpu.VMEM((2,) + block, F32),
            dma((8 + h,)),
            dma((h, 2, line)),
            dma((h, n_blk)),
            dma((h, n_rep)),
            dma((h, n_rep)),
            dma((h, n_rep)),
            dma((h, n_rep)),
            dma((h, 2, line)),
            dma((h, line)),
            dma((h, line)),
            dma((h,)),
            dma((5, max(line, n_rep))),
            dma((5, max(line, n_rep))),
        ],
        compiler_params=pltpu.CompilerParams(
            collective_id=0, has_side_effects=True, vmem_limit_bytes=62 * 1024 * 1024
        ),
    )(
        tile_row[0, 0], tile_col[0, 0], tile_count, tile_values[0, 0],
        node_features, weight, cotangent[0, 0],
    )
    layer, gw, gf = pl.pallas_call(
        hand_over,
        out_shape=results,
        in_specs=[anywhere] * 3,
        out_specs=(anywhere,) * 3,
        scratch_shapes=[pltpu.VMEM(made[i].shape, made[i].dtype) for i in range(3)] + [dma((2, 3))],
        compiler_params=pltpu.CompilerParams(vmem_limit_bytes=62 * 1024 * 1024),
    )(*made)
    return layer.reshape((1, 1) + block), gw, gf


def solution(mesh):
    placed = (
        P(("rep", "blk"), None),
        P("rep", "blk", None, None, None),
        P("rep", "blk", None),
        P("rep", "blk", None),
        P("rep", "blk"),
        P(),
        P("blk", "rep", None, None),
    )
    return jax.shard_map(
        functools.partial(on_device, mesh.shape["rep"], mesh.shape["blk"]),
        mesh=mesh,
        in_specs=placed,
        out_specs=(P("blk", "rep", None, None), P(), P(("rep", "blk"), None)),
        check_vma=False,
    )
```

```python
import functools

import jax
import jax.numpy as jnp
from jax import lax
from jax.experimental import pallas as pl
from jax.experimental.pallas import tpu as pltpu
from jax.sharding import PartitionSpec as P

MESH = pl.DeviceIdType.MESH
BF16, F32 = jnp.bfloat16, jnp.float32
PIECES = 2


def partner(index, step):
    out, bit = index, 1
    while bit <= step:
        if step & bit:
            out = out + bit * (1 - 2 * ((index // bit) % 2))
        bit *= 2
    return out


def kernel(
    n_rep, n_blk, pieces,
    row_ref, col_ref, count_ref, tiles_hbm, x_hbm, w_hbm, cot_hbm,
    layer_hbm, gw_hbm, gf_hbm,
    slot_vec, slot_ref, layer_ref, gw_ref, gf_ref,
    tiles, slabs, xg, w, cot, acc, pout, pin, gg, bsib_out, bsib_in, bout, bin_, brelay,
    wsib_out, wsib_in, wl_out, wl_in, wr_in, wgath, wpart, fin,
    loc, xs, xr, ps, pr, gs, gr, bs, br_sib, br_line, br_relay, ws, wr,
):
    rows, feats = x_hbm.shape
    tile = tiles.shape[1]
    dense, turned = slabs.at[0], slabs.at[slabs.shape[0] - 1]
    per = rows // tile
    line = n_blk // 2
    slab, group = rows * n_rep, rows * n_blk
    slab_blocks, group_blocks = slab // tile, group // tile
    fh = feats // pieces
    relay = line == 4
    r, b = lax.axis_index("rep"), lax.axis_index("blk")
    z, c = b // 2, b % 2
    other = b + 1 - 2 * c
    outer = jnp.logical_or(z == 0, z == line - 1)

    def blk_at(m):
        return partner(z, m) * 2 + c

    def remote(src, dst, send, recv, rep, blk):
        return pltpu.make_async_remote_copy(
            src_ref=src, dst_ref=dst, send_sem=send, recv_sem=recv,
            device_id={"rep": rep, "blk": blk}, device_id_type=MESH,
        )

    def arrive(dst, send, recv, rep, blk):
        remote(dst, dst, send, recv, rep, blk).wait_recv()

    fetch = [
        pltpu.make_async_copy(tiles_hbm, tiles.at[pl.ds(1, tiles.shape[0] - 1)], loc.at[1]),
        pltpu.make_async_copy(w_hbm, w, loc.at[2]),
        pltpu.make_async_copy(cot_hbm, cot, loc.at[3]),
    ]
    x_in = [
        pltpu.make_async_copy(x_hbm.at[:, pl.ds(h * fh, fh)], xg.at[b, h], loc.at[8 + h])
        for h in range(pieces)
    ]
    for copy in x_in + fetch:
        copy.start()

    barrier = pltpu.get_barrier_semaphore()
    friends = [(r, blk_at(m)) for m in range(1, line)] + [(r, other)]
    friends += [(partner(r, m), b) for m in range(1, n_rep)]
    for rep, blk in friends:
        pl.semaphore_signal(
            barrier, inc=1, device_id={"rep": rep, "blk": blk}, device_id_type=MESH
        )
    tiles[0] = jnp.zeros((tile, tile), BF16)

    shape = slot_vec.shape
    spots = lax.broadcasted_iota(jnp.int32, shape, 0) * shape[1] + lax.broadcasted_iota(
        jnp.int32, shape, 1
    )

    def mark(t, found):
        named = jnp.where(t < count_ref[0, 0], row_ref[t] * group_blocks + col_ref[t], -1)
        return jnp.where(spots == named, t + 1, found)

    slot_vec[...] = lax.fori_loop(
        0, row_ref.shape[0], mark, jnp.zeros(shape, jnp.int32), unroll=8
    )
    slots_in = pltpu.make_async_copy(slot_vec, slot_ref, loc.at[4])
    slots_in.start()
    pl.semaphore_wait(barrier, len(friends))

    def cols(h):
        return pl.ds(h * fh, fh)

    sends = []

    def x_line(h, m):
        return remote(
            xg.at[b, h], xg.at[b, h], xs.at[h, 0, m], xr.at[h, b], r, blk_at(m)
        )

    def x_relay(h):
        via = blk_at(2)
        return remote(
            xg.at[via, h], xg.at[via, h], xs.at[h, 0, 0], xr.at[h, via],
            r, blk_at(1),
        )

    def x_pass(h, m):
        blk = blk_at(m)
        src = xg.at[blk, h]
        return remote(
            src, xg.at[blk, h], xs.at[h, 1, m], xr.at[h, blk], r, other
        )

    for h in range(pieces):
        x_in[h].wait()
        for m in range(line - 1, 0, -1):
            if relay and m == 3:
                @pl.when(jnp.logical_not(outer))
                def _():
                    x_line(h, m).start()
            else:
                x_line(h, m).start()
        x_pass(h, 0).start()

    fetch[0].wait()
    slots_in.wait()

    def slot_at(pair):
        return slot_ref[pair // shape[1], pair % shape[1]]

    def lay_out(n, carry):
        panel, k = n // slab_blocks, n % slab_blocks
        for j in range(per):
            slot = slot_at(k * group_blocks + panel * per + j)
            start = pl.multiple_of(panel * slab + k * tile, tile)
            dense[pl.ds(start, tile), j * tile:(j + 1) * tile] = tiles[slot]
        return carry

    lax.fori_loop(0, n_blk * slab_blocks, lay_out, 0, unroll=8)

    def turn(t, carry):
        tiles[t] = tiles[t].T
        return carry

    def lay_out_turned(n, carry):
        panel, k = n // group_blocks, n % group_blocks
        for j in range(per):
            slot = slot_at((panel * per + j) * group_blocks + k)
            start = pl.multiple_of(panel * group + k * tile, tile)
            turned[pl.ds(start, tile), j * tile:(j + 1) * tile] = tiles[slot]
        return carry

    def steps(body, first, last, count, unroll):
        size = (last - first) // count
        return [
            functools.partial(
                lax.fori_loop, first + i * size, first + (i + 1) * size, body, 0, unroll=unroll
            )
            for i in range(count)
        ]

    later = steps(turn, 1, tiles.shape[0], 2, 4)
    later += steps(lay_out_turned, 0, n_rep * group_blocks, 4, 8)
    early = slabs.shape[0] > 1

    chunk = 4 * rows if slab % (4 * rows) == 0 else rows

    def add_panel(slabs, h, base, height, rhs, first):
        for at in range(0, height, chunk):
            lhs = slabs[pl.ds(pl.multiple_of(base + at, tile), chunk), :]
            part = jnp.dot(lhs, rhs, preferred_element_type=F32)
            if first:
                acc[pl.ds(at, chunk), cols(h)] = part
            else:
                acc[pl.ds(at, chunk), cols(h)] += part

    def p_send(h, m):
        to = partner(r, m)
        return remote(
            pout.at[to, h], pin.at[r, h], ps.at[h, m], pr.at[h, r], to, b
        )

    span = min(n_blk, 8)

    def partial_rows(h, to):
        def add(first, total):
            for i in range(span):
                blk = first * span + i
                at = pl.multiple_of(blk * slab + to * rows, rows)
                total += jnp.dot(
                    dense[pl.ds(at, rows), :], xg[blk, h], preferred_element_type=F32
                )
            return total

        zero = jnp.zeros((rows, fh), F32)
        return add(0, zero) if span == n_blk else lax.fori_loop(0, n_blk // span, add, zero)

    for h in range(pieces):
        arrive(xg.at[other, h], xs.at[h, 1, 0], xr.at[h, other], r, other)
        for m in range(1, line):
            blk = blk_at(m)
            arrive(xg.at[blk, h], xs.at[h, 0, m], xr.at[h, blk], r, blk)
            if relay and m == 2:
                @pl.when(jnp.logical_not(outer))
                def _():
                    x_relay(h).start()
            x_pass(h, m).start()
            if early and later and h == 0:
                later.pop(0)()
                later.pop(0)()
        for m in range(1, line):
            last = partner(z, m) * 2 + 1 - c
            arrive(xg.at[last, h], xs.at[h, 1, m], xr.at[h, last], r, other)
        for m in range(n_rep - 1, -1, -1):
            to = partner(r, m)
            pout[to, h] = partial_rows(h, to).astype(BF16)
            if m:
                p_send(h, m).start()

    while later:
        later.pop(0)()
    fetch[1].wait()
    fetch[2].wait()

    hidden, preact = [], 0.0
    for h in range(pieces):
        total = pout[r, h].astype(F32)
        for m in range(1, n_rep):
            peer = partner(r, m)
            arrive(pin.at[peer, h], ps.at[h, m], pr.at[h, peer], peer, b)
            total = total + pin[peer, h].astype(F32)
        hidden.append(total.astype(BF16))
        preact += jnp.dot(hidden[h], w[cols(h), :], preferred_element_type=F32)
    gate = jax.nn.sigmoid(preact)
    slope = gate * (1.0 + preact * (1.0 - gate))
    grad_pre = (cot[...].astype(F32) * slope).astype(BF16)

    def g_send(h, m):
        to = partner(r, m)
        return remote(
            gg.at[r, h], gg.at[r, h], gs.at[h, m], gr.at[h, r], to, b
        )

    for h in range(pieces):
        gg[r, h] = lax.dot_general(
            grad_pre, w[cols(h), :], (((1,), (1,)), ((), ())), preferred_element_type=F32
        ).astype(BF16)
        for m in range(n_rep - 1, 0, -1):
            g_send(h, m).start()

    layer_ref[...] = (preact * gate).astype(BF16)
    layer_out = pltpu.make_async_copy(layer_ref, layer_hbm, loc.at[5])
    layer_out.start()
    for h in range(pieces):
        wpart[cols(h), :] = lax.dot_general(
            hidden[h], grad_pre, (((0,), (0,)), ((), ())), preferred_element_type=F32
        )
    half = feats // 2
    share = half // line
    kind = wl_out.dtype
    mine_at, other_at = c * half, (1 - c) * half
    wsib_out[...] = wpart[pl.ds(pl.multiple_of(other_at, half), half), :].astype(kind)
    w_sib = remote(wsib_out, wsib_in, ws.at[0, 0], wr.at[0, 0], r, other)
    w_sib.start()

    add_panel(turned, 0, r * group, group, gg[r, 0], True)

    w_sib.wait_recv()
    both = wpart[pl.ds(pl.multiple_of(mine_at, half), half), :] + wsib_in[...].astype(F32)
    wpart[pl.ds(0, half), :] = both
    for m in range(line):
        at = pl.multiple_of(partner(z, m) * share, share)
        wl_out[m] = wpart[pl.ds(at, share), :].astype(kind)

    def w_line(m):
        return remote(wl_out.at[m], wl_in.at[m], ws.at[1, m], wr.at[1, m], r, blk_at(m))

    for m in range(1, line):
        w_line(m).start()

    def w_rep(m):
        return remote(
            wr_in.at[r], wr_in.at[r], ws.at[2, m], wr.at[2, r], partner(r, m), b
        )

    def w_sum_line():
        part = wl_out[0].astype(F32)
        for m in range(1, line):
            w_line(m).wait_recv()
            part = part + wl_in[m].astype(F32)
        wr_in[r] = part.astype(kind)
        for m in range(1, n_rep):
            w_rep(m).start()

    def w_back(m):
        return remote(
            wgath.at[c, z], wgath.at[c, z], ws.at[3, m], wr.at[3, z], r, blk_at(m)
        )

    def w_pass(m):
        place = partner(z, m)
        return remote(
            wgath.at[c, place], wgath.at[c, place], ws.at[4, m], wr.at[4, place], r, other
        )

    def w_sum_rep():
        for m in range(1, n_rep):
            peer = partner(r, m)
            arrive(wr_in.at[peer], ws.at[2, m], wr.at[2, peer], peer, b)
        part = wr_in[0].astype(F32)
        for i in range(1, n_rep):
            part = part + wr_in[i].astype(F32)
        wgath[c, z] = part.astype(kind)
        for m in range(1, line):
            w_back(m).start()
        w_pass(0).start()

    def b_sib(h, m):
        place = partner(z, m)
        return remote(
            bsib_out.at[place, h], bsib_in.at[place, h],
            bs.at[h, 0, m], br_sib.at[h, place], r, other,
        )

    def b_line(h, m):
        return remote(
            bout.at[m, h], bin_.at[m, h],
            bs.at[h, 1, m], br_line.at[h, m], r, blk_at(m),
        )

    def b_relay(h):
        return remote(
            bout.at[3, h], brelay.at[h],
            bs.at[h, 1, 3], br_relay.at[h], r, blk_at(2),
        )

    tail = n_rep - 1

    def finish(h, blk):
        peer = partner(r, tail)
        at = pl.multiple_of(blk * rows, rows)
        if h == 0:
            panel = turned[pl.ds(pl.multiple_of(peer * group + blk * rows, rows), rows), :]
            return acc[pl.ds(at, rows), cols(h)] + jnp.dot(
                panel, gg[peer, h], preferred_element_type=F32
            )
        total = jnp.zeros((rows, fh), F32)
        for rep in range(n_rep):
            panel = turned[pl.ds(pl.multiple_of(rep * group + blk * rows, rows), rows), :]
            total += jnp.dot(panel, gg[rep, h], preferred_element_type=F32)
        return total

    def back_terms(h):
        for m in range(1, n_rep):
            peer = partner(r, m)
            arrive(gg.at[peer, h], gs.at[h, m], gr.at[h, peer], peer, b)
            if m < tail and h == 0:
                add_panel(turned, h, peer * group, group, gg[peer, h], False)
        for m in range(line - 1, -1, -1):
            place = partner(z, m)
            bsib_out[place, h] = finish(h, place * 2 + 1 - c).astype(BF16)
            b_sib(h, m).start()

    def chip_sum(h, m):
        place = partner(z, m)
        mine = finish(h, place * 2 + c)
        arrive(bsib_in.at[place, h], bs.at[h, 0, m], br_sib.at[h, place], r, other)
        return mine + bsib_in[place, h].astype(F32)

    def send_far(h):
        for m in range(line - 1, 1, -1):
            bout[m, h] = chip_sum(h, m).astype(BF16)
            if relay and m == 3:
                @pl.when(outer)
                def _():
                    b_relay(h).start()

                @pl.when(jnp.logical_not(outer))
                def _():
                    b_line(h, m).start()
            else:
                b_line(h, m).start()
        fin[1, :, cols(h)] = chip_sum(h, 1)
        fin[0, :, cols(h)] = chip_sum(h, 0)

    def send_near(h):
        if relay:
            @pl.when(jnp.logical_not(outer))
            def _():
                b_relay(h).wait_recv()
                fin[1, :, cols(h)] += brelay[h].astype(F32)

        bout[1, h] = fin[1, :, cols(h)].astype(BF16)
        b_line(h, 1).start()

    for h in range(pieces):
        back_terms(h)
        if h == 0:
            w_sum_line()
        else:
            send_near(h - 1)
        if h == pieces - 1:
            w_sum_rep()
        send_far(h)
    send_near(pieces - 1)

    for m in range(1, line):
        place = partner(z, m)
        arrive(wgath.at[c, place], ws.at[3, m], wr.at[3, place], r, blk_at(m))
        w_pass(m).start()
    for m in range(line):
        place = partner(z, m)
        arrive(wgath.at[1 - c, place], ws.at[4, m], wr.at[4, place], r, other)
    for core in range(2):
        for place in range(line):
            at = core * half + place * share
            gw_ref[at:at + share, :] = wgath[core, place].astype(F32)
    gw_out = pltpu.make_async_copy(gw_ref, gw_hbm, loc.at[6])
    gw_out.start()

    for h in range(pieces):
        for m in range(1, line):
            if relay and m == 3:
                @pl.when(jnp.logical_not(outer))
                def _():
                    b_line(h, m).wait_recv()
                    fin[0, :, cols(h)] += bin_[m, h].astype(F32)
            else:
                b_line(h, m).wait_recv()
                fin[0, :, cols(h)] += bin_[m, h].astype(F32)
    gf_ref[...] = fin[0].astype(BF16)
    gf_out = pltpu.make_async_copy(gf_ref, gf_hbm, loc.at[7])
    gf_out.start()

    for h in range(pieces):
        for m in range(1, line):
            if relay and m == 3:
                @pl.when(jnp.logical_not(outer))
                def _():
                    x_line(h, m).wait_send()
                    x_relay(h).wait_send()
            else:
                x_line(h, m).wait_send()
            b_line(h, m).wait_send()
        for m in range(line):
            x_pass(h, m).wait_send()
            b_sib(h, m).wait_send()
        for m in range(1, n_rep):
            p_send(h, m).wait_send()
            g_send(h, m).wait_send()
    w_sib.wait_send()
    for m in range(1, line):
        w_line(m).wait_send()
        w_back(m).wait_send()
    for m in range(line):
        w_pass(m).wait_send()
    for m in range(1, n_rep):
        w_rep(m).wait_send()


    for copy in (layer_out, gw_out, gf_out):
        copy.wait()


def hand_over(layer, gw, gf, layer_to, gw_to, gf_to, layer_at, gw_at, gf_at, sems):
    trips = [(layer, layer_at, layer_to), (gw, gw_at, gw_to), (gf, gf_at, gf_to)]
    inward = [pltpu.make_async_copy(a, b, sems.at[0, i]) for i, (a, b, _) in enumerate(trips)]
    outward = [pltpu.make_async_copy(b, c, sems.at[1, i]) for i, (_, b, c) in enumerate(trips)]
    for copy in inward:
        copy.start()
    for first, second in zip(inward, outward):
        first.wait()
        second.start()
    for copy in outward:
        copy.wait()


def on_device(n_rep, n_blk, node_features, tile_values, tile_row, tile_col, tile_count, weight, cotangent):
    rows, feats = node_features.shape
    slots, tile = tile_values.shape[2], tile_values.shape[3]
    slab_blocks = n_rep * rows // tile
    group_blocks = n_blk * rows // tile
    line = n_blk // 2
    share = feats // 2 // line
    kind = BF16 if share % 16 == 0 else F32
    pairs = slab_blocks * group_blocks
    table = (-(-pairs // 1024) * 8, 128)
    block = (rows, feats)
    h = PIECES
    piece = (h, rows, feats // h)
    slab_size = n_blk * n_rep * rows
    copies = 2 if slab_size * rows * 4 <= 24 * 1024 * 1024 else 1
    dma = pltpu.SemaphoreType.DMA
    results = (
        jax.ShapeDtypeStruct(block, BF16),
        jax.ShapeDtypeStruct((feats, feats), F32),
        jax.ShapeDtypeStruct(block, BF16),
    )
    anywhere = pl.BlockSpec(memory_space=pl.ANY)
    scalars = pl.BlockSpec(memory_space=pltpu.SMEM)
    made = pl.pallas_call(
        functools.partial(kernel, n_rep, n_blk, h),
        out_shape=results,
        in_specs=[scalars] * 3 + [anywhere] * 4,
        out_specs=(anywhere,) * 3,
        scratch_shapes=[
            pltpu.VMEM(table, jnp.int32),
            pltpu.SMEM(table, jnp.int32),
            pltpu.VMEM(block, BF16),
            pltpu.VMEM((feats, feats), F32),
            pltpu.VMEM(block, BF16),
            pltpu.VMEM((slots + 1, tile, tile), BF16),
            pltpu.VMEM((copies, slab_size, rows), BF16),
            pltpu.VMEM((n_blk,) + piece, BF16),
            pltpu.VMEM((feats, feats), BF16),
            pltpu.VMEM(block, BF16),
            pltpu.VMEM((max(n_blk, n_rep) * rows, feats), F32),
            pltpu.VMEM((n_rep,) + piece, BF16),
            pltpu.VMEM((n_rep,) + piece, BF16),
            pltpu.VMEM((n_rep,) + piece, BF16),
            pltpu.VMEM((line,) + piece, BF16),
            pltpu.VMEM((line,) + piece, BF16),
            pltpu.VMEM((line,) + piece, BF16),
            pltpu.VMEM((line,) + piece, BF16),
            pltpu.VMEM(piece, BF16),
            pltpu.VMEM((feats // 2, feats), kind),
            pltpu.VMEM((feats // 2, feats), kind),
            pltpu.VMEM((line, share, feats), kind),
            pltpu.VMEM((line, share, feats), kind),
            pltpu.VMEM((n_rep, share, feats), kind),
            pltpu.VMEM((2, line, share, feats), kind),
            pltpu.VMEM((feats, feats), F32),
            pltpu.VMEM((2,) + block, F32),
            dma((8 + h,)),
            dma((h, 2, line)),
            dma((h, n_blk)),
            dma((h, n_rep)),
            dma((h, n_rep)),
            dma((h, n_rep)),
            dma((h, n_rep)),
            dma((h, 2, line)),
            dma((h, line)),
            dma((h, line)),
            dma((h,)),
            dma((5, max(line, n_rep))),
            dma((5, max(line, n_rep))),
        ],
        compiler_params=pltpu.CompilerParams(
            collective_id=0, has_side_effects=True, vmem_limit_bytes=62 * 1024 * 1024
        ),
    )(
        tile_row[0, 0], tile_col[0, 0], tile_count, tile_values[0, 0],
        node_features, weight, cotangent[0, 0],
    )
    layer, gw, gf = pl.pallas_call(
        hand_over,
        out_shape=results,
        in_specs=[anywhere] * 3,
        out_specs=(anywhere,) * 3,
        scratch_shapes=[pltpu.VMEM(made[i].shape, made[i].dtype) for i in range(3)] + [dma((2, 3))],
        compiler_params=pltpu.CompilerParams(vmem_limit_bytes=62 * 1024 * 1024),
    )(*made)
    return layer.reshape((1, 1) + block), gw, gf


def solution(mesh):
    placed = (
        P(("rep", "blk"), None),
        P("rep", "blk", None, None, None),
        P("rep", "blk", None),
        P("rep", "blk", None),
        P("rep", "blk"),
        P(),
        P("blk", "rep", None, None),
    )
    return jax.shard_map(
        functools.partial(on_device, mesh.shape["rep"], mesh.shape["blk"]),
        mesh=mesh,
        in_specs=placed,
        out_specs=(P("blk", "rep", None, None), P(), P(("rep", "blk"), None)),
        check_vma=False,
    )
```

```python
import functools

import jax
import jax.numpy as jnp
from jax import lax
from jax.experimental import pallas as pl
from jax.experimental.pallas import tpu as pltpu
from jax.sharding import PartitionSpec as P

MESH = pl.DeviceIdType.MESH
BF16, F32 = jnp.bfloat16, jnp.float32
PIECES = 2


def partner(index, step):
    out, bit = index, 1
    while bit <= step:
        if step & bit:
            out = out + bit * (1 - 2 * ((index // bit) % 2))
        bit *= 2
    return out


def kernel(
    n_rep, n_blk, pieces,
    row_ref, col_ref, count_ref, tiles_hbm, x_hbm, w_hbm, cot_hbm,
    layer_hbm, gw_hbm, gf_hbm,
    slot_vec, slot_ref, layer_ref, gw_ref, gf_ref,
    tiles, slabs, xg, w, cot, acc, pout, pin, gg, bsib_out, bsib_in, bout, bin_, brelay,
    wsib_out, wsib_in, wl_out, wl_in, wr_in, wgath, wpart, fin,
    loc, xs, xr, ps, pr, gs, gr, bs, br_sib, br_line, br_relay, ws, wr,
):
    rows, feats = x_hbm.shape
    tile = tiles.shape[1]
    dense, turned = slabs.at[0], slabs.at[slabs.shape[0] - 1]
    per = rows // tile
    line = n_blk // 2
    slab, group = rows * n_rep, rows * n_blk
    slab_blocks, group_blocks = slab // tile, group // tile
    fh = feats // pieces
    relay = line == 4
    r, b = lax.axis_index("rep"), lax.axis_index("blk")
    z, c = b // 2, b % 2
    other = b + 1 - 2 * c
    outer = jnp.logical_or(z == 0, z == line - 1)

    def blk_at(m):
        return partner(z, m) * 2 + c

    def remote(src, dst, send, recv, rep, blk):
        return pltpu.make_async_remote_copy(
            src_ref=src, dst_ref=dst, send_sem=send, recv_sem=recv,
            device_id={"rep": rep, "blk": blk}, device_id_type=MESH,
        )

    def arrive(dst, send, recv, rep, blk):
        remote(dst, dst, send, recv, rep, blk).wait_recv()

    fetch = [
        pltpu.make_async_copy(tiles_hbm, tiles.at[pl.ds(1, tiles.shape[0] - 1)], loc.at[1]),
        pltpu.make_async_copy(w_hbm, w, loc.at[2]),
        pltpu.make_async_copy(cot_hbm, cot, loc.at[3]),
    ]
    x_in = [
        pltpu.make_async_copy(x_hbm.at[:, pl.ds(h * fh, fh)], xg.at[b, h], loc.at[8 + h])
        for h in range(pieces)
    ]
    for copy in x_in + fetch:
        copy.start()

    barrier = pltpu.get_barrier_semaphore()
    friends = [(r, blk_at(m)) for m in range(1, line)] + [(r, other)]
    friends += [(partner(r, m), b) for m in range(1, n_rep)]
    for rep, blk in friends:
        pl.semaphore_signal(
            barrier, inc=1, device_id={"rep": rep, "blk": blk}, device_id_type=MESH
        )
    tiles[0] = jnp.zeros((tile, tile), BF16)

    shape = slot_vec.shape
    spots = lax.broadcasted_iota(jnp.int32, shape, 0) * shape[1] + lax.broadcasted_iota(
        jnp.int32, shape, 1
    )

    def mark(t, found):
        named = jnp.where(t < count_ref[0, 0], row_ref[t] * group_blocks + col_ref[t], -1)
        return jnp.where(spots == named, t + 1, found)

    slot_vec[...] = lax.fori_loop(
        0, row_ref.shape[0], mark, jnp.zeros(shape, jnp.int32), unroll=8
    )
    slots_in = pltpu.make_async_copy(slot_vec, slot_ref, loc.at[4])
    slots_in.start()
    pl.semaphore_wait(barrier, len(friends))

    def cols(h):
        return pl.ds(h * fh, fh)

    sends = []

    def x_line(h, m):
        return remote(
            xg.at[b, h], xg.at[b, h], xs.at[h, 0, m], xr.at[h, b], r, blk_at(m)
        )

    def x_relay(h):
        via = blk_at(2)
        return remote(
            xg.at[via, h], xg.at[via, h], xs.at[h, 0, 0], xr.at[h, via],
            r, blk_at(1),
        )

    def x_pass(h, m):
        blk = blk_at(m)
        src = xg.at[blk, h]
        return remote(
            src, xg.at[blk, h], xs.at[h, 1, m], xr.at[h, blk], r, other
        )

    for h in range(pieces):
        x_in[h].wait()
        for m in range(line - 1, 0, -1):
            if relay and m == 3:
                @pl.when(jnp.logical_not(outer))
                def _():
                    x_line(h, m).start()
            else:
                x_line(h, m).start()
        x_pass(h, 0).start()

    fetch[0].wait()
    slots_in.wait()

    def slot_at(pair):
        return slot_ref[pair // shape[1], pair % shape[1]]

    def lay_out(n, carry):
        panel, k = n // slab_blocks, n % slab_blocks
        for j in range(per):
            slot = slot_at(k * group_blocks + panel * per + j)
            start = pl.multiple_of(panel * slab + k * tile, tile)
            dense[pl.ds(start, tile), j * tile:(j + 1) * tile] = tiles[slot]
        return carry

    lax.fori_loop(0, n_blk * slab_blocks, lay_out, 0, unroll=8)

    def turn(t, carry):
        tiles[t] = tiles[t].T
        return carry

    def lay_out_turned(n, carry):
        panel, k = n // group_blocks, n % group_blocks
        for j in range(per):
            slot = slot_at((panel * per + j) * group_blocks + k)
            start = pl.multiple_of(panel * group + k * tile, tile)
            turned[pl.ds(start, tile), j * tile:(j + 1) * tile] = tiles[slot]
        return carry

    def steps(body, first, last, count, unroll):
        size = (last - first) // count
        return [
            functools.partial(
                lax.fori_loop, first + i * size, first + (i + 1) * size, body, 0, unroll=unroll
            )
            for i in range(count)
        ]

    lax.fori_loop(1, tiles.shape[0], turn, 0, unroll=4)
    later = steps(lay_out_turned, 0, n_rep * group_blocks, 4, 8)

    chunk = 4 * rows if slab % (4 * rows) == 0 else rows

    def add_panel(slabs, h, base, height, rhs, first):
        for at in range(0, height, chunk):
            lhs = slabs[pl.ds(pl.multiple_of(base + at, tile), chunk), :]
            part = jnp.dot(lhs, rhs, preferred_element_type=F32)
            if first:
                acc[pl.ds(at, chunk), cols(h)] = part
            else:
                acc[pl.ds(at, chunk), cols(h)] += part

    def p_send(h, m):
        to = partner(r, m)
        return remote(
            pout.at[to, h], pin.at[r, h], ps.at[h, m], pr.at[h, r], to, b
        )

    span = min(n_blk, 8)

    def partial_rows(h, to):
        def add(first, total):
            for i in range(span):
                blk = first * span + i
                at = pl.multiple_of(blk * slab + to * rows, rows)
                total += jnp.dot(
                    dense[pl.ds(at, rows), :], xg[blk, h], preferred_element_type=F32
                )
            return total

        zero = jnp.zeros((rows, fh), F32)
        return add(0, zero) if span == n_blk else lax.fori_loop(0, n_blk // span, add, zero)

    for h in range(pieces):
        arrive(xg.at[other, h], xs.at[h, 1, 0], xr.at[h, other], r, other)
        for m in range(1, line):
            blk = blk_at(m)
            arrive(xg.at[blk, h], xs.at[h, 0, m], xr.at[h, blk], r, blk)
            if relay and m == 2:
                @pl.when(jnp.logical_not(outer))
                def _():
                    x_relay(h).start()
            x_pass(h, m).start()
        for m in range(1, line):
            last = partner(z, m) * 2 + 1 - c
            arrive(xg.at[last, h], xs.at[h, 1, m], xr.at[h, last], r, other)
        for m in range(n_rep - 1, -1, -1):
            to = partner(r, m)
            pout[to, h] = partial_rows(h, to).astype(BF16)
            if m:
                p_send(h, m).start()

    while later:
        later.pop(0)()
    fetch[1].wait()
    fetch[2].wait()

    hidden, preact = [], 0.0
    for h in range(pieces):
        total = pout[r, h].astype(F32)
        for m in range(1, n_rep):
            peer = partner(r, m)
            arrive(pin.at[peer, h], ps.at[h, m], pr.at[h, peer], peer, b)
            total = total + pin[peer, h].astype(F32)
        hidden.append(total.astype(BF16))
        preact += jnp.dot(hidden[h], w[cols(h), :], preferred_element_type=F32)
    gate = jax.nn.sigmoid(preact)
    slope = gate * (1.0 + preact * (1.0 - gate))
    grad_pre = (cot[...].astype(F32) * slope).astype(BF16)

    def g_send(h, m):
        to = partner(r, m)
        return remote(
            gg.at[r, h], gg.at[r, h], gs.at[h, m], gr.at[h, r], to, b
        )

    for h in range(pieces):
        gg[r, h] = lax.dot_general(
            grad_pre, w[cols(h), :], (((1,), (1,)), ((), ())), preferred_element_type=F32
        ).astype(BF16)
        for m in range(n_rep - 1, 0, -1):
            g_send(h, m).start()

    layer_ref[...] = (preact * gate).astype(BF16)
    layer_out = pltpu.make_async_copy(layer_ref, layer_hbm, loc.at[5])
    layer_out.start()
    for h in range(pieces):
        wpart[cols(h), :] = lax.dot_general(
            hidden[h], grad_pre, (((0,), (0,)), ((), ())), preferred_element_type=F32
        )
    half = feats // 2
    share = half // line
    kind = wl_out.dtype
    mine_at, other_at = c * half, (1 - c) * half
    wsib_out[...] = wpart[pl.ds(pl.multiple_of(other_at, half), half), :].astype(kind)
    w_sib = remote(wsib_out, wsib_in, ws.at[0, 0], wr.at[0, 0], r, other)
    w_sib.start()

    add_panel(turned, 0, r * group, group, gg[r, 0], True)

    w_sib.wait_recv()
    both = wpart[pl.ds(pl.multiple_of(mine_at, half), half), :] + wsib_in[...].astype(F32)
    wpart[pl.ds(0, half), :] = both
    for m in range(line):
        at = pl.multiple_of(partner(z, m) * share, share)
        wl_out[m] = wpart[pl.ds(at, share), :].astype(kind)

    def w_line(m):
        return remote(wl_out.at[m], wl_in.at[m], ws.at[1, m], wr.at[1, m], r, blk_at(m))

    for m in range(1, line):
        w_line(m).start()

    def w_rep(m):
        return remote(
            wr_in.at[r], wr_in.at[r], ws.at[2, m], wr.at[2, r], partner(r, m), b
        )

    def w_sum_line():
        part = wl_out[0].astype(F32)
        for m in range(1, line):
            w_line(m).wait_recv()
            part = part + wl_in[m].astype(F32)
        wr_in[r] = part.astype(kind)
        for m in range(1, n_rep):
            w_rep(m).start()

    def w_back(m):
        return remote(
            wgath.at[c, z], wgath.at[c, z], ws.at[3, m], wr.at[3, z], r, blk_at(m)
        )

    def w_pass(m):
        place = partner(z, m)
        return remote(
            wgath.at[c, place], wgath.at[c, place], ws.at[4, m], wr.at[4, place], r, other
        )

    def w_sum_rep():
        for m in range(1, n_rep):
            peer = partner(r, m)
            arrive(wr_in.at[peer], ws.at[2, m], wr.at[2, peer], peer, b)
        part = wr_in[0].astype(F32)
        for i in range(1, n_rep):
            part = part + wr_in[i].astype(F32)
        wgath[c, z] = part.astype(kind)
        for m in range(1, line):
            w_back(m).start()
        w_pass(0).start()

    def b_sib(h, m):
        place = partner(z, m)
        return remote(
            bsib_out.at[place, h], bsib_in.at[place, h],
            bs.at[h, 0, m], br_sib.at[h, place], r, other,
        )

    def b_line(h, m):
        return remote(
            bout.at[m, h], bin_.at[m, h],
            bs.at[h, 1, m], br_line.at[h, m], r, blk_at(m),
        )

    def b_relay(h):
        return remote(
            bout.at[3, h], brelay.at[h],
            bs.at[h, 1, 3], br_relay.at[h], r, blk_at(2),
        )

    tail = n_rep - 1

    def finish(h, blk):
        peer = partner(r, tail)
        at = pl.multiple_of(blk * rows, rows)
        if h == 0:
            panel = turned[pl.ds(pl.multiple_of(peer * group + blk * rows, rows), rows), :]
            return acc[pl.ds(at, rows), cols(h)] + jnp.dot(
                panel, gg[peer, h], preferred_element_type=F32
            )
        total = jnp.zeros((rows, fh), F32)
        for rep in range(n_rep):
            panel = turned[pl.ds(pl.multiple_of(rep * group + blk * rows, rows), rows), :]
            total += jnp.dot(panel, gg[rep, h], preferred_element_type=F32)
        return total

    def back_terms(h):
        for m in range(1, n_rep):
            peer = partner(r, m)
            arrive(gg.at[peer, h], gs.at[h, m], gr.at[h, peer], peer, b)
            if m < tail and h == 0:
                add_panel(turned, h, peer * group, group, gg[peer, h], False)
        for m in range(line - 1, -1, -1):
            place = partner(z, m)
            bsib_out[place, h] = finish(h, place * 2 + 1 - c).astype(BF16)
            b_sib(h, m).start()

    def chip_sum(h, m):
        place = partner(z, m)
        mine = finish(h, place * 2 + c)
        arrive(bsib_in.at[place, h], bs.at[h, 0, m], br_sib.at[h, place], r, other)
        return mine + bsib_in[place, h].astype(F32)

    def send_far(h):
        for m in range(line - 1, 1, -1):
            bout[m, h] = chip_sum(h, m).astype(BF16)
            if relay and m == 3:
                @pl.when(outer)
                def _():
                    b_relay(h).start()

                @pl.when(jnp.logical_not(outer))
                def _():
                    b_line(h, m).start()
            else:
                b_line(h, m).start()
        fin[1, :, cols(h)] = chip_sum(h, 1)
        fin[0, :, cols(h)] = chip_sum(h, 0)

    def send_near(h):
        if relay:
            @pl.when(jnp.logical_not(outer))
            def _():
                b_relay(h).wait_recv()
                fin[1, :, cols(h)] += brelay[h].astype(F32)

        bout[1, h] = fin[1, :, cols(h)].astype(BF16)
        b_line(h, 1).start()

    for h in range(pieces):
        back_terms(h)
        if h == 0:
            w_sum_line()
        else:
            send_near(h - 1)
        if h == pieces - 1:
            w_sum_rep()
        send_far(h)
    send_near(pieces - 1)

    for m in range(1, line):
        place = partner(z, m)
        arrive(wgath.at[c, place], ws.at[3, m], wr.at[3, place], r, blk_at(m))
        w_pass(m).start()
    for m in range(line):
        place = partner(z, m)
        arrive(wgath.at[1 - c, place], ws.at[4, m], wr.at[4, place], r, other)
    for core in range(2):
        for place in range(line):
            at = core * half + place * share
            gw_ref[at:at + share, :] = wgath[core, place].astype(F32)
    gw_out = pltpu.make_async_copy(gw_ref, gw_hbm, loc.at[6])
    gw_out.start()

    for h in range(pieces):
        for m in range(1, line):
            if relay and m == 3:
                @pl.when(jnp.logical_not(outer))
                def _():
                    b_line(h, m).wait_recv()
                    fin[0, :, cols(h)] += bin_[m, h].astype(F32)
            else:
                b_line(h, m).wait_recv()
                fin[0, :, cols(h)] += bin_[m, h].astype(F32)
    gf_ref[...] = fin[0].astype(BF16)
    gf_out = pltpu.make_async_copy(gf_ref, gf_hbm, loc.at[7])
    gf_out.start()

    for h in range(pieces):
        for m in range(1, line):
            if relay and m == 3:
                @pl.when(jnp.logical_not(outer))
                def _():
                    x_line(h, m).wait_send()
                    x_relay(h).wait_send()
            else:
                x_line(h, m).wait_send()
            b_line(h, m).wait_send()
        for m in range(line):
            x_pass(h, m).wait_send()
            b_sib(h, m).wait_send()
        for m in range(1, n_rep):
            p_send(h, m).wait_send()
            g_send(h, m).wait_send()
    w_sib.wait_send()
    for m in range(1, line):
        w_line(m).wait_send()
        w_back(m).wait_send()
    for m in range(line):
        w_pass(m).wait_send()
    for m in range(1, n_rep):
        w_rep(m).wait_send()


    for copy in (layer_out, gw_out, gf_out):
        copy.wait()


def hand_over(layer, gw, gf, layer_to, gw_to, gf_to, layer_at, gw_at, gf_at, sems):
    trips = [(layer, layer_at, layer_to), (gw, gw_at, gw_to), (gf, gf_at, gf_to)]
    inward = [pltpu.make_async_copy(a, b, sems.at[0, i]) for i, (a, b, _) in enumerate(trips)]
    outward = [pltpu.make_async_copy(b, c, sems.at[1, i]) for i, (_, b, c) in enumerate(trips)]
    for copy in inward:
        copy.start()
    for first, second in zip(inward, outward):
        first.wait()
        second.start()
    for copy in outward:
        copy.wait()


def on_device(n_rep, n_blk, node_features, tile_values, tile_row, tile_col, tile_count, weight, cotangent):
    rows, feats = node_features.shape
    slots, tile = tile_values.shape[2], tile_values.shape[3]
    slab_blocks = n_rep * rows // tile
    group_blocks = n_blk * rows // tile
    line = n_blk // 2
    share = feats // 2 // line
    kind = BF16 if share % 16 == 0 else F32
    pairs = slab_blocks * group_blocks
    table = (-(-pairs // 1024) * 8, 128)
    block = (rows, feats)
    h = PIECES
    piece = (h, rows, feats // h)
    slab_size = n_blk * n_rep * rows
    copies = 2 if slab_size * rows * 4 <= 24 * 1024 * 1024 else 1
    dma = pltpu.SemaphoreType.DMA
    results = (
        jax.ShapeDtypeStruct(block, BF16),
        jax.ShapeDtypeStruct((feats, feats), F32),
        jax.ShapeDtypeStruct(block, BF16),
    )
    anywhere = pl.BlockSpec(memory_space=pl.ANY)
    scalars = pl.BlockSpec(memory_space=pltpu.SMEM)
    made = pl.pallas_call(
        functools.partial(kernel, n_rep, n_blk, h),
        out_shape=results,
        in_specs=[scalars] * 3 + [anywhere] * 4,
        out_specs=(anywhere,) * 3,
        scratch_shapes=[
            pltpu.VMEM(table, jnp.int32),
            pltpu.SMEM(table, jnp.int32),
            pltpu.VMEM(block, BF16),
            pltpu.VMEM((feats, feats), F32),
            pltpu.VMEM(block, BF16),
            pltpu.VMEM((slots + 1, tile, tile), BF16),
            pltpu.VMEM((copies, slab_size, rows), BF16),
            pltpu.VMEM((n_blk,) + piece, BF16),
            pltpu.VMEM((feats, feats), BF16),
            pltpu.VMEM(block, BF16),
            pltpu.VMEM((max(n_blk, n_rep) * rows, feats), F32),
            pltpu.VMEM((n_rep,) + piece, BF16),
            pltpu.VMEM((n_rep,) + piece, BF16),
            pltpu.VMEM((n_rep,) + piece, BF16),
            pltpu.VMEM((line,) + piece, BF16),
            pltpu.VMEM((line,) + piece, BF16),
            pltpu.VMEM((line,) + piece, BF16),
            pltpu.VMEM((line,) + piece, BF16),
            pltpu.VMEM(piece, BF16),
            pltpu.VMEM((feats // 2, feats), kind),
            pltpu.VMEM((feats // 2, feats), kind),
            pltpu.VMEM((line, share, feats), kind),
            pltpu.VMEM((line, share, feats), kind),
            pltpu.VMEM((n_rep, share, feats), kind),
            pltpu.VMEM((2, line, share, feats), kind),
            pltpu.VMEM((feats, feats), F32),
            pltpu.VMEM((2,) + block, F32),
            dma((8 + h,)),
            dma((h, 2, line)),
            dma((h, n_blk)),
            dma((h, n_rep)),
            dma((h, n_rep)),
            dma((h, n_rep)),
            dma((h, n_rep)),
            dma((h, 2, line)),
            dma((h, line)),
            dma((h, line)),
            dma((h,)),
            dma((5, max(line, n_rep))),
            dma((5, max(line, n_rep))),
        ],
        compiler_params=pltpu.CompilerParams(
            collective_id=0, has_side_effects=True, vmem_limit_bytes=62 * 1024 * 1024
        ),
    )(
        tile_row[0, 0], tile_col[0, 0], tile_count, tile_values[0, 0],
        node_features, weight, cotangent[0, 0],
    )
    layer, gw, gf = pl.pallas_call(
        hand_over,
        out_shape=results,
        in_specs=[anywhere] * 3,
        out_specs=(anywhere,) * 3,
        scratch_shapes=[pltpu.VMEM(made[i].shape, made[i].dtype) for i in range(3)] + [dma((2, 3))],
        compiler_params=pltpu.CompilerParams(vmem_limit_bytes=62 * 1024 * 1024),
    )(*made)
    return layer.reshape((1, 1) + block), gw, gf


def solution(mesh):
    placed = (
        P(("rep", "blk"), None),
        P("rep", "blk", None, None, None),
        P("rep", "blk", None),
        P("rep", "blk", None),
        P("rep", "blk"),
        P(),
        P("blk", "rep", None, None),
    )
    return jax.shard_map(
        functools.partial(on_device, mesh.shape["rep"], mesh.shape["blk"]),
        mesh=mesh,
        in_specs=placed,
        out_specs=(P("blk", "rep", None, None), P(), P(("rep", "blk"), None)),
        check_vma=False,
    )
```
